32 devices in a mesh: ctx: 8 (over z, y), exp: 4 (over x, core).
Axes of the slice: x: 2, y: 2, z: 4, core: 2. Of those that a mesh axis runs over, the one named last changes fastest.
Arguments:
- activations: bfloat16 [4, 1024, 768], P('exp', 'ctx'), may hold values from -6 to 6
- gain_one: bfloat16 [768], P(('ctx', 'exp')), may hold values from 0.5 to 1.5
- query_key_value_weight: bfloat16 [768, 2304], P(('ctx', 'exp')), may hold values from -0.21875 to 0.21875
- attention_output_weight: bfloat16 [768, 768], P(('ctx', 'exp')), may hold values from -3.5 to 3.5
- pos_table: float32 [32, 12], replicated, may hold values from -3 to 3
- gain_two: bfloat16 [768], P(('ctx', 'exp')), may hold values from 0.5 to 1.5
- w_router: bfloat16 [768, 4], P(('ctx', 'exp')), may hold values from -0.15625 to 0.15625
- w_in: bfloat16 [4, 768, 3072], P('exp', 'ctx'), may hold values from -0.21875 to 0.21875
- w_out: bfloat16 [4, 3072, 768], P('exp', 'ctx'), may hold values from -0.109375 to 0.109375
- routes: int32 [4, 1024, 2], P('exp', 'ctx'), may hold values from 0 to 3, all different within a row; in each aligned block of 128 rows (0 to 127, 128 to 255, ..., all dimensions but the last counted through in order) at most 80 rows name the same one
- pair_of_device: int32 [8], replicated, may hold values from 0 to 7, each once
- cotangent: float32 [4, 1024, 768], P('exp', 'ctx'), may hold values from -6 to 6
Outputs:
- output: float32 [4, 1024, 768], P('exp', 'ctx')
- d_activations: float32 [4, 1024, 768], P('exp', 'ctx')
- d_gain_one: float32 [768], P(('ctx', 'exp'))
- d_w_qkv: float32 [768, 2304], P(('ctx', 'exp'))
- d_w_attn_out: float32 [768, 768], P(('ctx', 'exp'))
- d_pos_table: float32 [32, 12], replicated
- d_gain_two: float32 [768], P(('ctx', 'exp'))
- d_w_router: float32 [768, 4], P(('ctx', 'exp'))
- d_w_in: float32 [4, 768, 3072], P('exp', 'ctx')
- d_w_out: float32 [4, 3072, 768], P('exp', 'ctx')
The draws below stay inside these ranges and needn't reach their ends.
Inputs may be any that keep to these rules, and one draw needn't show every extreme that they name: `routes`: A token names 2 different experts. In each aligned block of 128 stored rows of a sequence (the rows of one device) no expert is named by more than 80 rows, a bound that some block reaches. `pair_of_device`: each value appears once.
All inputs are finite; a program needn't handle non-finite values.
Results may differ from the reference program's by a relative error of at most 0.015.
Values may be sent and summed in bfloat16 or wider, within the bound.
No kernel may reach another device: no remote copies, remote signals or barrier semaphores. Data moves between devices by JAX's collectives and lax.ppermute only.
A program may use at most 192 MiB of HBM per device.

```python
import math
import jax
import jax.numpy as jnp
import numpy as np
from jax import lax

D = 768
HEADS = 12
HEAD_DIM = 64
FF = 3072
NB = 32
TOPK = 2
CTX_TOK = 128
EXPERTS = 4
SEQS = 4
SEQ_LEN = 1024
CAP = 80
N_CTX = 8


def block_levels(own_key, dims, pieces, low, largest):
    level = 1.0
    for axis_at, shards_of in pieces:
        steps = jax.random.uniform(jax.random.fold_in(jax.random.fold_in(own_key, 6), axis_at), (shards_of,), jnp.float32, low / len(pieces), largest / len(pieces))
        level = level * jnp.repeat(jnp.exp(steps), dims[axis_at] // shards_of).reshape((-1,) + (1,) * (len(dims) - 1 - axis_at))
    return level


def deal_out(key, own, number, rows, number_of, top, limit, lean):
    sequence = jax.random.permutation(key, number_of)
    crowded, common = shares(number_of, rows * top, limit, lean, True), shares(number_of, rows * top, limit, lean, False)
    places = jnp.arange(number_of)

    def named(tallies, turn):
        used = int((tallies > 0).sum())
        fixed = max(1, used // 4)
        passed = fixed + (places - fixed + turn * (used - fixed)) % max(1, number_of - fixed)
        return jnp.zeros((number_of,), jnp.int32).at[sequence[jnp.where(places < fixed, places, passed)]].set(jnp.asarray(tallies, jnp.int32))

    tallies = jnp.where(number % 4 == 0, named(crowded, number // 4), named(common, number - number // 4 - 1))
    mixed = jax.random.permutation(jax.random.fold_in(own, 3), number_of)
    source_of, sink = mixed[0:number_of // 2 * 2:2], mixed[1:number_of // 2 * 2:2]
    margin = jnp.minimum(tallies[source_of] - 1, limit - tallies[sink]) // 2
    margin = jnp.where((source_of == sequence[0]) | (sink == sequence[0]) | (tallies[sink] == 0), 0, jnp.maximum(margin, 0))
    passed = jax.random.randint(jax.random.fold_in(own, 4), (number_of // 2,), 0, 1 << 20) % (margin + 1)
    tallies = tallies.at[source_of].add(-passed).at[sink].add(passed)
    items = jnp.searchsorted(jnp.cumsum(tallies), jnp.arange(rows * top), side="right").astype(jnp.int32)
    grid = items.reshape(top, rows).T
    grid = grid[jax.random.permutation(jax.random.fold_in(own, 1), rows)]
    turn = jax.random.randint(jax.random.fold_in(own, 2), (rows, 1), 0, top)
    return jnp.take_along_axis(grid, (jnp.arange(top)[None, :] + turn) % top, axis=1)


def shares(amount, total, limit, slope, full):
    portions = [(1 << 20) // math.isqrt(grade ** slope) + 1 for grade in range(1, amount + 1)]
    largest = limit if full else min(limit, max(-(-total // amount), total * portions[0] // sum(portions)))
    least = 1 if total - largest >= amount - 1 else 0
    given, rest = [largest] + [least] * (amount - 1), total - largest - least * (amount - 1)
    while rest > 0:
        candidates = [i for i in range(1, amount) if given[i] < largest] or [i for i in range(1, amount) if given[i] < limit]
        pool, left = sum([portions[i] for i in candidates]), rest
        for i in candidates:
            extra = min(limit - given[i], max(1, left * portions[i] // pool), rest)
            given[i] = given[i] + extra
            rest = rest - extra
    return np.array(given)


def scatter_about(rng, extent, width, bound, pieces=(), kind=jnp.bfloat16):
    drawn = width * jax.random.normal(rng, extent, jnp.float32)
    if pieces:
        drawn = drawn * block_levels(rng, extent, pieces, -0.22, 0.18)
    return jnp.clip(drawn, -bound, bound).astype(kind)


def setup_inputs(seed: int = 0) -> dict:
    splits = jax.random.split(jax.random.key(seed), 13)
    activations = scatter_about(splits[0], (SEQS, SEQ_LEN, D), 1.0, 6.0, ((0, 4), (1, 8)))
    gain_one = jnp.clip(1.0 + 0.1 * jax.random.normal(splits[1], (D,), jnp.float32), 0.5, 1.5).astype(jnp.bfloat16)
    query_key_value_weight = scatter_about(splits[2], (D, 3 * D), D ** -0.5, 0.21875, ((0, 32),))
    attention_output_weight = scatter_about(splits[3], (D, D), (max(1, 4 * D // SEQ_LEN)) ** -0.5, 3.5, ((0, 32),))
    pos_table = scatter_about(splits[4], (NB, HEADS), 0.5, 3.0, (), jnp.float32)
    gain_two = jnp.clip(1.0 + 0.1 * jax.random.normal(splits[5], (D,), jnp.float32), 0.5, 1.5).astype(jnp.bfloat16)
    w_router = scatter_about(splits[6], (D, EXPERTS), (2 * D) ** -0.5, 0.15625, ((0, 32),))
    w_in = scatter_about(splits[7], (EXPERTS, D, FF), D ** -0.5, 0.21875, ((0, 4), (1, 8)))
    w_out = scatter_about(splits[8], (EXPERTS, FF, D), FF ** -0.5, 0.109375, ((0, 4), (1, 8)))
    routes_keys = jax.random.split(jax.random.fold_in(splits[9], 1), SEQS * SEQ_LEN // CTX_TOK)
    routes_turns = jax.random.permutation(jax.random.fold_in(splits[9], 3), SEQS * SEQ_LEN // CTX_TOK)
    routes = jax.vmap(lambda own, number: deal_out(jax.random.fold_in(splits[9], 2), own, number, CTX_TOK, EXPERTS, TOPK, CAP, 2))(routes_keys, routes_turns).reshape((SEQS, SEQ_LEN, TOPK))
    pair_of_device = jax.random.permutation(splits[10], N_CTX).astype(jnp.int32)
    cotangent = scatter_about(splits[11], (SEQS, SEQ_LEN, D), 1.0, 6.0, ((0, 4), (1, 8)), jnp.float32)
    return {"activations": activations, "gain_one": gain_one, "query_key_value_weight": query_key_value_weight, "attention_output_weight": attention_output_weight, "pos_table": pos_table, "gain_two": gain_two, "w_router": w_router, "w_in": w_in, "w_out": w_out, "routes": routes, "pair_of_device": pair_of_device, "cotangent": cotangent}


PRECISION_FULL = lax.Precision.HIGHEST

@jax.custom_vjp
def reduced_precision(v):
    return lax.optimization_barrier(v.astype(jnp.bfloat16)).astype(jnp.float32)

@jax.custom_vjp
def reduced_backward(v):
    return v

def low_keep(v):
    return (reduced_precision(v), None)

def low_pass(kept, grad):
    return (grad,)

def back_keep(v):
    return (v, None)

def back_low(kept, grad):
    return (reduced_precision(grad),)
reduced_precision.defvjp(low_keep, low_pass)
reduced_backward.defvjp(back_keep, back_low)

def rms_norm(values, gain):
    scale = lax.rsqrt(lax.optimization_barrier(jnp.mean(values * values, axis=-1, keepdims=True)) + 1e-06)
    return values * scale * gain

def stored_positions(pair_of_device):
    half_width = CTX_TOK // 2
    row_index = jnp.arange(N_CTX * CTX_TOK, dtype=jnp.int32)
    owner = row_index // CTX_TOK
    within = row_index % CTX_TOK
    first_block = pair_of_device[owner]
    block_index = jnp.where(within < half_width, first_block, 2 * N_CTX - 1 - first_block)
    return (block_index * half_width + within % half_width).astype(jnp.int32)

def attend_rows(queries, key_rows, value_rows, query_pos, key_pos, bias_table):
    half_width = CTX_TOK // 2
    scores = jnp.einsum('qhe,khe->hqk', queries, key_rows, precision=PRECISION_FULL) * 0.125
    bucket = jnp.clip(query_pos[:, None] // half_width - key_pos[None, :] // half_width, 0, NB - 1)
    scores = scores + jnp.transpose(bias_table[bucket], (2, 0, 1))
    scores = reduced_backward(scores)
    visible = query_pos[:, None] >= key_pos[None, :]
    scores = jnp.where(visible[None], scores, -1e+30)
    weights = jax.nn.softmax(scores, axis=-1)
    return jnp.einsum('hqk,khe->qhe', reduced_precision(weights), value_rows, precision=PRECISION_FULL)

def attend_sequence(queries, key_rows, value_rows, positions, bias_table):
    block_rows = math.gcd(512, SEQ_LEN)
    count = SEQ_LEN // block_rows
    query_blocks = queries.reshape(count, block_rows, HEADS, HEAD_DIM)
    position_blocks = positions.reshape(count, block_rows)

    def one_block(entries):
        return attend_rows(entries[0], key_rows, value_rows, entries[1], positions, bias_table)
    mixed_blocks = lax.map(jax.checkpoint(one_block), (query_blocks, position_blocks))
    return mixed_blocks.reshape(SEQ_LEN, HEADS * HEAD_DIM)

def forward(inputs, gain_one, query_key_value_weight, attention_output_weight, pos_table, gain_two, w_router, w_in, w_out, routes, positions):
    first_normalized = reduced_precision(rms_norm(inputs, gain_one))
    query_key_value = reduced_precision(reduced_backward(jnp.einsum('vbk,kr->vbr', first_normalized, query_key_value_weight, precision=PRECISION_FULL)))
    queries = query_key_value[..., :D].reshape(SEQS, SEQ_LEN, HEADS, HEAD_DIM)
    key_rows = query_key_value[..., D:2 * D].reshape(SEQS, SEQ_LEN, HEADS, HEAD_DIM)
    value_rows = query_key_value[..., 2 * D:].reshape(SEQS, SEQ_LEN, HEADS, HEAD_DIM)

    def one_sequence(entries):
        return attend_sequence(entries[0], entries[1], entries[2], positions, pos_table)
    merged_head_output = lax.map(jax.checkpoint(one_sequence), (queries, key_rows, value_rows))
    merged_head_output = reduced_precision(reduced_backward(merged_head_output))
    attention_result = reduced_backward(jnp.einsum('puw,wb->pub', merged_head_output, attention_output_weight, precision=PRECISION_FULL))
    resid = inputs + attention_result
    normed_two = reduced_precision(rms_norm(resid, gain_two))
    token_rows = normed_two.reshape(-1, D)
    router_logits = jnp.dot(token_rows, w_router, precision=PRECISION_FULL)
    expert_ids = routes.reshape(-1, TOPK)
    chosen = jnp.take_along_axis(router_logits, expert_ids, axis=1)
    gate_weights = jax.nn.softmax(chosen, axis=-1)
    block_count = SEQS * N_CTX
    block_ids = expert_ids.reshape(block_count, CTX_TOK * TOPK)
    hits = (block_ids[..., None] == jnp.arange(EXPERTS, dtype=jnp.int32)).astype(jnp.int32)
    slot_rank = lax.optimization_barrier(jnp.sum((jnp.cumsum(hits, axis=1) - hits) * hits, axis=-1))
    block_base = jnp.arange(block_count, dtype=jnp.int32)[:, None] * CAP
    target = (block_ids * (block_count * CAP) + block_base + slot_rank).reshape(-1).astype(jnp.int32)
    copies = reduced_backward(jnp.repeat(token_rows, TOPK, axis=0))
    buffer = jnp.zeros((EXPERTS * block_count * CAP, D), jnp.float32).at[target].add(copies)
    buffer = buffer.reshape(EXPERTS, block_count * CAP, D)

    def one_expert(entries):
        rows, first_proj, second_proj = entries
        hidden = reduced_backward(jnp.dot(rows, first_proj, precision=PRECISION_FULL))
        active = reduced_precision(jax.nn.gelu(hidden))
        return reduced_precision(reduced_backward(jnp.dot(active, second_proj, precision=PRECISION_FULL)))
    answers = lax.map(jax.checkpoint(one_expert), (buffer, w_in, w_out)).reshape(-1, D)
    picked = answers[target].reshape(-1, TOPK, D)
    expert_sum = lax.optimization_barrier(jnp.sum(gate_weights[..., None] * picked, axis=1))
    return resid + expert_sum.reshape(SEQS, SEQ_LEN, D)

def reference(activations, gain_one, query_key_value_weight, attention_output_weight, pos_table, gain_two, w_router, w_in, w_out, routes, pair_of_device, cotangent):
    positions = stored_positions(pair_of_device)
    floats = (activations, gain_one, query_key_value_weight, attention_output_weight, pos_table, gain_two, w_router, w_in, w_out)
    floats = tuple((item.astype(jnp.float32) for item in floats))

    def wrapped(inputs, gain_a, qkv_w, attn_w, table_w, gain_b, router_w, first_w, second_w):
        return forward(inputs, gain_a, qkv_w, attn_w, table_w, gain_b, router_w, first_w, second_w, routes, positions)
    output, pullback = jax.vjp(wrapped, *floats)
    grads = pullback(cotangent.astype(jnp.float32))
    return (output, grads[0], grads[1], grads[2], grads[3], grads[4], grads[5], grads[6], grads[7], grads[8])
```

```python
import jax
import jax.numpy as jnp
from jax import lax
from jax.sharding import Mesh, PartitionSpec as P

PRECISION_FULL = lax.Precision.HIGHEST
MASKED = -1e30
LOW = jnp.bfloat16
WIDE = jnp.float32
EPS = 1e-06


def dot(left, right, contract):
    return lax.dot_general(left, right, (contract, ((), ())), preferred_element_type=WIDE)


def shift(x, axis, d):
    n = lax.axis_size(axis)
    return lax.ppermute(x, axis, [((j + d) % n, j) for j in range(n)])


def swap(x, axes, k):
    n = 1
    for axis in axes:
        n *= lax.axis_size(axis)
    return lax.ppermute(x, axes, [(j ^ k, j) for j in range(n)])


def from_xor(blocks, me):
    step = 1
    while step < len(blocks):
        flip = (me & step) != 0
        blocks = [jnp.where(flip, blocks[j ^ step], blocks[j]) for j in range(len(blocks))]
        step *= 2
    return blocks


def from_cyclic(blocks, me):
    n, step = len(blocks), 1
    while step < n:
        move = (me & step) != 0
        blocks = [jnp.where(move, blocks[(j - step) % n], blocks[j]) for j in range(n)]
        step *= 2
    return blocks


def pick(stack, index):
    return lax.dynamic_index_in_dim(stack, index, 0, keepdims=False)


def layer_gather(block):
    yx_count = lax.axis_size("yy") * lax.axis_size("xx")
    me_yx = lax.axis_index("yy") * lax.axis_size("xx") + lax.axis_index("xx")
    blocks = [block] + [swap(block, ("yy", "xx"), k) for k in range(1, yx_count)]
    joined = jnp.stack(from_xor(blocks, me_yx))
    both = from_xor([joined, swap(joined, ("cc",), 1)], lax.axis_index("cc"))
    full = jnp.stack(both)
    cores, layers, outer, rows, width = full.shape
    return full.transpose(2, 1, 0, 3, 4).reshape(outer * layers * cores * rows, width)


def layer_reduce(part):
    outer, yx = lax.axis_size("hz"), lax.axis_size("yy") * lax.axis_size("xx")
    me_yx = lax.axis_index("yy") * lax.axis_size("xx") + lax.axis_index("xx")
    cores = lax.axis_size("cc")
    me_c = lax.axis_index("cc")
    rows = part.shape[0] // (outer * yx * cores)
    split = part.reshape(outer, yx, cores, rows, part.shape[1]).transpose(2, 1, 0, 3, 4)
    other = swap(pick(split, 1 - me_c).astype(LOW), ("cc",), 1)
    mine = pick(split, me_c).astype(WIDE) + other.astype(WIDE)
    low = mine.astype(LOW)
    total = pick(mine, me_yx)
    for k in range(1, yx):
        total = total + swap(pick(low, me_yx ^ k), ("yy", "xx"), k).astype(WIDE)
    return total


def line_gather(block):
    n = lax.axis_size("hz")
    right, left = block, block
    from_left, from_right = [None] * n, [None] * n
    for s in range(1, n):
        right = lax.ppermute(right, "hz", [(i, i + 1) for i in range(s - 1, n - 1)])
        left = lax.ppermute(left, "hz", [(i, i - 1) for i in range(1, n - s + 1)])
        from_left[s], from_right[s] = right, left
    return [block] + [from_right[d] + from_left[n - d] for d in range(1, n)]


def line_reduce(blocks):
    n = lax.axis_size("hz")
    right = left = None
    for s in range(1, n):
        send_right, send_left = blocks[n - s], blocks[s]
        if s > 1:
            send_right = (send_right.astype(WIDE) + right.astype(WIDE)).astype(LOW)
            send_left = (send_left.astype(WIDE) + left.astype(WIDE)).astype(LOW)
        right = lax.ppermute(send_right, "hz", [(i, i + 1) for i in range(s)])
        left = lax.ppermute(send_left, "hz", [(i, i - 1) for i in range(n - s, n)])
    return blocks[0].astype(WIDE) + right.astype(WIDE) + left.astype(WIDE)


def three_terms(x):
    high = lax.reduce_precision(x, 8, 7)
    rest = x - high
    middle = lax.reduce_precision(rest, 8, 7)
    return high.astype(LOW), middle.astype(LOW), (rest - middle).astype(LOW)


def body(
    activations,
    gain_one,
    query_key_value_weight,
    attention_output_weight,
    pos_table,
    gain_two,
    w_router,
    w_in,
    w_out,
    routes,
    pair_of_device,
    cotangent,
):
    Z, Y = lax.axis_size("hz"), lax.axis_size("yy")
    X, C = lax.axis_size("xx"), lax.axis_size("cc")
    E, N = X * C, Z * Y
    z, y = lax.axis_index("hz"), lax.axis_index("yy")
    me_e = lax.axis_index("xx") * C + lax.axis_index("cc")
    _, own_rows, D = activations.shape
    half = own_rows // 2
    buckets, heads = pos_table.shape
    hd = D // heads
    hg = heads // Z
    gw = hg * hd
    top = routes.shape[2]
    shard = gain_one.shape[0]
    FF = w_in.shape[2]
    capacity = max(2, 5 * own_rows * top // (4 * E))

    acts = activations[0]
    act_blocks = [acts] + [shift(acts, "hz", d) for d in range(1, Z)]
    qkv_w = query_key_value_weight.reshape(shard, 3, Z, gw).transpose(2, 0, 1, 3)
    small = jnp.concatenate([gain_one[:, None], gain_two[:, None], w_router], axis=1)
    small_width = -(-(gw + small.shape[1]) // 128) * 128 - gw
    small = jnp.pad(small, ((0, 0), (0, small_width - small.shape[1])))
    small = jnp.broadcast_to(small[None], (Z, shard, small_width))
    payload = jnp.concatenate([qkv_w[:, :, 1], qkv_w[:, :, 2], qkv_w[:, :, 0], small], axis=-1)
    pieces = [pick(payload, z)] + [
        shift(pick(payload, (z - d) % Z), "hz", d) for d in range(1, Z)
    ]
    w_all = layer_gather(jnp.stack(from_cyclic(pieces, z)))

    w_in_split = w_in[0].reshape(D // N, Z, Y, FF // N).transpose(2, 0, 1, 3)
    w_in_split = w_in_split.reshape(Y, D // N, FF // Y)
    in_rows = [pick(w_in_split, y)] + [
        swap(pick(w_in_split, y ^ k), ("yy",), k) for k in range(1, Y)
    ]
    in_rows = jnp.concatenate(from_xor(in_rows, y), axis=0)
    in_blocks = line_gather(in_rows)
    out_blocks = line_gather(w_out[0])

    def place(blocks):
        rows = blocks[0].shape[0]
        whole = jnp.zeros((Z * rows, blocks[0].shape[1]), LOW)
        for d in range(Z):
            whole = lax.dynamic_update_slice(whole, blocks[d], (((z + d) % Z) * rows, 0))
        return whole

    attn_w_pieces = [attention_output_weight] + [
        shift(attention_output_weight, "hz", d) for d in range(1, Z)
    ]
    w_attn_out = layer_gather(jnp.stack(from_cyclic(attn_w_pieces, z)))

    gain_first = w_all[:, 3 * gw].astype(WIDE)
    gain_second = w_all[:, 3 * gw + 1].astype(WIDE)
    router = w_all[:, 3 * gw + 2 : 3 * gw + 2 + E]

    def first_of(owner):
        lanes = lax.broadcasted_iota(jnp.int32, (N,), 0)
        return jnp.sum(jnp.where(lanes == owner, pair_of_device, 0))

    def tiles_of(k):
        found = []
        for d in range(Z):
            first = first_of(((z + d) % Z) * Y + (y ^ k))
            found += [first, 2 * N - 1 - first]
        return found

    key_tile_list = [t for k in range(Y) for t in tiles_of(k)]
    key_tiles = jnp.stack(key_tile_list)
    query_tiles = key_tiles[: 2 * Z]
    n_q, n_k = 2 * Z, 2 * Z * Y
    within = lax.broadcasted_iota(jnp.int32, (1, half), 1)
    query_pos = (query_tiles[:, None] * half + within).reshape(-1)
    key_pos = (key_tiles[:, None] * half + within).reshape(-1)
    bucket = jnp.clip(query_tiles[:, None] - key_tiles[None, :], 0, buckets - 1)
    levels = lax.broadcasted_iota(jnp.int32, (n_q, n_k, buckets), 2)
    bucket_hot = bucket[:, :, None] == levels
    own_table = lax.dynamic_slice(pos_table, (0, z * hg), (buckets, hg)).T
    tile_bias = jnp.sum(jnp.where(bucket_hot[None], own_table[:, None, None, :], 0.0), axis=-1)
    bias_terms = jnp.concatenate(three_terms(tile_bias), axis=-1)
    bias_rows = jnp.broadcast_to(
        bias_terms[:, :, None, :], (hg, n_q, half, 3 * n_k)
    ).reshape(hg, n_q * half, 3 * n_k)
    key_hot = (
        lax.broadcasted_iota(jnp.int32, (n_k * half, n_k), 0) // half
        == lax.broadcasted_iota(jnp.int32, (n_k * half, n_k), 1)
    ).astype(LOW)

    x_rows = jnp.concatenate(act_blocks, axis=0).astype(WIDE)
    scale_one = lax.rsqrt(jnp.mean(x_rows * x_rows, axis=-1, keepdims=True) + EPS)
    hat_one = x_rows * scale_one
    normed_one = (hat_one * gain_first).astype(LOW)
    w_kv, w_q = w_all[:, : 2 * gw], w_all[:, 2 * gw : 3 * gw]
    kv = dot(normed_one, w_kv, ((1,), (0,))).astype(LOW)
    kv_all = jnp.concatenate([kv] + [swap(kv, ("yy",), k) for k in range(1, Y)], axis=0)
    q = dot(normed_one, w_q, ((1,), (0,))).astype(LOW)

    def by_head(rows):
        return rows.reshape(rows.shape[0], hg, hd).transpose(1, 0, 2)

    q_heads = by_head(q) * jnp.asarray(hd**-0.5, LOW)
    k_heads, v_heads = by_head(kv_all[:, :gw]), by_head(kv_all[:, gw:])
    q_wide = jnp.concatenate([q_heads, bias_rows], axis=-1)
    k_hot = jnp.broadcast_to(key_hot[None], (hg,) + key_hot.shape)
    k_wide = jnp.concatenate([k_heads, k_hot, k_hot, k_hot], axis=-1)
    scores = jnp.einsum("hqe,hke->hqk", q_wide, k_wide, preferred_element_type=WIDE)
    visible = query_pos[:, None] >= key_pos[None, :]
    scores = jnp.where(visible[None], scores, MASKED)
    weights = jnp.exp(scores - jnp.max(scores, axis=-1, keepdims=True))
    probs = weights / jnp.sum(weights, axis=-1, keepdims=True)
    probs_low = probs.astype(LOW)
    mixed_heads = jnp.einsum("hqk,hke->qhe", probs_low, v_heads, preferred_element_type=WIDE)
    mixed = mixed_heads.reshape(Z, own_rows, gw).astype(LOW)
    mixed_back = [mixed[0]] + [shift(mixed[d], "hz", -d) for d in range(1, Z)]
    mixed_back = from_cyclic([mixed_back[-d % Z] for d in range(Z)], z)
    mixed_full = jnp.concatenate(mixed_back, axis=-1)

    own_x = acts.astype(WIDE)
    resid = own_x + dot(mixed_full, w_attn_out, ((1,), (0,)))
    scale_two = lax.rsqrt(jnp.mean(resid * resid, axis=-1, keepdims=True) + EPS)
    hat_two = resid * scale_two
    normed_two = (hat_two * gain_second).astype(LOW)

    relative = routes[0] ^ me_e
    flat = relative.reshape(own_rows * top)
    expert_iota = lax.broadcasted_iota(jnp.int32, (1, E), 1)
    hits = (flat[:, None] == expert_iota).astype(LOW)
    earlier = (
        lax.broadcasted_iota(jnp.int32, (own_rows * top, own_rows * top), 0)
        > lax.broadcasted_iota(jnp.int32, (own_rows * top, own_rows * top), 1)
    ).astype(LOW)
    before = dot(earlier, hits, ((1,), (0,)))
    rank = jnp.sum(before * hits.astype(WIDE), axis=-1).astype(jnp.int32)
    target = flat * capacity + rank
    slot_iota = lax.broadcasted_iota(jnp.int32, (1, E * capacity), 1)
    route_map = (target[:, None] == slot_iota).astype(LOW)
    per_token = route_map.reshape(own_rows, top, E * capacity).sum(axis=1)
    chosen_mask = (routes[0][..., None] == expert_iota[None]).astype(WIDE)

    group = ("yy", "xx", "cc")

    def exchange(slots):
        blocks = slots.reshape(E, capacity, slots.shape[1])
        got = [
            blocks[k] if j == 0 and k == 0 else swap(blocks[k], group, j * E + k)
            for j in range(Y)
            for k in range(E)
        ]
        return jnp.concatenate(got, axis=0)

    def give_back(rows):
        blocks = rows.reshape(Y, E, capacity, rows.shape[1])
        summed = []
        for k in range(E):
            total = None
            for j in range(Y):
                block = blocks[j, k]
                if j or k:
                    block = swap(block, group, j * E + k)
                block = block.astype(WIDE)
                total = block if total is None else total + block
            summed.append(total.astype(LOW))
        return jnp.concatenate(summed, axis=0)

    rows = exchange(dot(per_token, normed_two, ((0,), (0,))).astype(LOW))
    router_logits = dot(normed_two, router, ((1,), (0,)))
    chosen = jnp.sum(chosen_mask * router_logits[:, None, :], axis=-1)
    gates = jax.nn.softmax(chosen, axis=-1)
    cot = cotangent[0]
    grad_picked = (gates[..., None] * cot[:, None, :]).astype(LOW)
    grad_picked = grad_picked.reshape(own_rows * top, D)
    grad_rows = exchange(dot(route_map, grad_picked, ((0,), (0,))).astype(LOW))

    w_first, w_second = place(in_blocks), place(out_blocks)
    hidden = dot(rows, w_first, ((1,), (0,)))
    active, gelu_back = jax.vjp(jax.nn.gelu, hidden)
    active = active.astype(LOW)
    answer = dot(active, w_second, ((1,), (0,))).astype(LOW)
    grad_active = dot(grad_rows, w_second, ((1,), (1,)))
    grad_hidden = gelu_back(grad_active)[0].astype(LOW)
    grad_copy = dot(grad_hidden, w_first, ((1,), (1,))).astype(LOW)
    returned = give_back(answer)
    coming = give_back(grad_copy)

    part_ff, part_d = FF // N, D // Z
    grad_out_blocks = [
        dot(
            lax.dynamic_slice_in_dim(active, ((z + d) % Z) * part_ff, part_ff, 1),
            grad_rows,
            ((0,), (0,)),
        ).astype(LOW)
        for d in range(Z)
    ]
    rows_t = rows.T
    grad_in_blocks = [
        dot(
            lax.dynamic_slice_in_dim(rows_t, ((z + d) % Z) * part_d, part_d, 0),
            grad_hidden,
            ((1,), (0,)),
        ).astype(LOW)
        for d in range(Z)
    ]

    picked = dot(route_map, returned, ((1,), (0,))).reshape(own_rows, top, D)
    output = resid + jnp.sum(gates[..., None] * picked, axis=1)
    grad_gates = jnp.sum(picked * cot[:, None, :], axis=-1)
    grad_chosen = gates * (grad_gates - jnp.sum(gates * grad_gates, axis=-1, keepdims=True))
    logit_gradient = jnp.sum(grad_chosen[..., None] * chosen_mask, axis=1)
    grad_normed_two = dot(per_token, coming, ((1,), (0,))) + jnp.einsum(
        "te,de->td", logit_gradient, router.astype(WIDE), precision=PRECISION_FULL
    )
    grad_router = jnp.einsum(
        "td,te->de", normed_two.astype(WIDE), logit_gradient, precision=PRECISION_FULL
    )
    grad_gain_two = jnp.sum(grad_normed_two * hat_two, axis=0)
    grad_hat = grad_normed_two * gain_second
    grad_resid = cot + scale_two * (
        grad_hat - hat_two * jnp.mean(grad_hat * hat_two, axis=-1, keepdims=True)
    )
    grad_attention = grad_resid.astype(LOW)
    grad_attn_out = dot(mixed_full, grad_attention, ((0,), (0,)))
    grad_mixed = lax.dot_general(
        w_attn_out.reshape(Z, gw, D),
        grad_attention,
        (((2,), (1,)), ((), ())),
        preferred_element_type=WIDE,
    ).transpose(0, 2, 1).astype(LOW)
    grad_mixed_rows = jnp.concatenate(
        [pick(grad_mixed, z)]
        + [shift(pick(grad_mixed, (z - d) % Z), "hz", d) for d in range(1, Z)],
        axis=0,
    )

    grad_heads = by_head(grad_mixed_rows)
    row_dot = jnp.sum(
        by_head(mixed.reshape(Z * own_rows, gw)).astype(WIDE) * grad_heads.astype(WIDE),
        axis=-1,
        keepdims=True,
    )
    grad_probs = jnp.einsum("hqe,hke->hqk", grad_heads, v_heads, preferred_element_type=WIDE)
    grad_scores = (probs_low.astype(WIDE) * (grad_probs - row_dot)).astype(LOW)
    grad_q_wide = jnp.einsum(
        "hqk,hke->hqe",
        grad_scores,
        jnp.concatenate([k_heads, k_hot], axis=-1),
        preferred_element_type=WIDE,
    )
    grad_q = grad_q_wide[..., :hd] * hd**-0.5
    tile_sums = grad_q_wide[..., hd:].reshape(hg, n_q, half, n_k).sum(axis=2)
    table_part = jnp.sum(
        jnp.where(bucket_hot[None], tile_sums[..., None], 0.0), axis=(1, 2)
    )
    grad_k = jnp.einsum("hqk,hqe->khe", grad_scores, q_heads, preferred_element_type=WIDE)
    grad_v = jnp.einsum("hqk,hqe->khe", probs_low, grad_heads, preferred_element_type=WIDE)
    grad_kv = jnp.concatenate(
        [grad_k.reshape(-1, gw), grad_v.reshape(-1, gw)], axis=1
    ).reshape(Y, Z * own_rows, 2 * gw)
    grad_kv_own = grad_kv[0]
    for k in range(1, Y):
        grad_kv_own = grad_kv_own + swap(grad_kv[k].astype(LOW), ("yy",), k).astype(WIDE)
    grad_q_rows = grad_q.transpose(1, 0, 2).reshape(-1, gw)
    grad_qkv = jnp.concatenate([grad_kv_own, grad_q_rows], axis=1).astype(LOW)

    grad_normed_part = dot(grad_qkv, w_all[:, : 3 * gw], ((1,), (1,)))
    grad_gain_one = jnp.sum(grad_normed_part * hat_one, axis=0)
    grad_low = grad_normed_part.astype(LOW).reshape(Z, own_rows, D)
    grad_normed_one = grad_normed_part[:own_rows]
    for d in range(1, Z):
        grad_normed_one = grad_normed_one + shift(grad_low[d], "hz", -d).astype(WIDE)
    own_hat = hat_one[:own_rows]
    grad_hat_one = grad_normed_one * gain_first
    grad_inputs = grad_resid + scale_one[:own_rows] * (
        grad_hat_one - own_hat * jnp.mean(grad_hat_one * own_hat, axis=-1, keepdims=True)
    )

    def pad_columns(columns):
        return jnp.pad(columns, ((0, 0), (0, 128 - columns.shape[1])))

    attn_part = jnp.concatenate(
        [grad_attn_out, pad_columns(jnp.concatenate([grad_gain_two[:, None], grad_router], 1))],
        axis=1,
    )
    attn_sum = layer_reduce(attn_part)
    attn_low = attn_sum.astype(LOW)
    attn_total = pick(attn_sum, z)
    for d in range(1, Z):
        attn_total = attn_total + shift(pick(attn_low, (z - d) % Z), "hz", d).astype(WIDE)
    shard_attn_out = attn_total[:, :D]
    shard_gain_two = attn_total[:, D]
    shard_router = attn_total[:, D + 1 : D + 1 + E]

    grad_w_qkv = dot(normed_one, grad_qkv, ((0,), (0,)))
    qkv_part = jnp.concatenate([grad_w_qkv, pad_columns(grad_gain_one[:, None])], axis=1)
    qkv_sum = layer_reduce(qkv_part)
    qkv_low = qkv_sum.astype(LOW)
    qkv_blocks = [pick(qkv_sum, z)] + [
        shift(pick(qkv_low, (z - d) % Z), "hz", d).astype(WIDE) for d in range(1, Z)
    ]
    shard_gain_one = sum(block[:, 3 * gw] for block in qkv_blocks)
    by_group = jnp.stack(from_cyclic([block[:, : 3 * gw] for block in qkv_blocks], z))
    by_group = by_group.reshape(Z, shard, 3, gw)
    shard_qkv = jnp.concatenate(
        [
            by_group[:, :, part].transpose(1, 0, 2).reshape(shard, D)
            for part in (2, 0, 1)
        ],
        axis=1,
    )

    table_sum = table_part
    table_sum = table_sum + swap(table_sum, ("cc",), 1)
    yx = ("yy", "xx")
    parts = [table_sum] + [swap(table_sum, yx, k) for k in range(1, Y * X)]
    parts = from_xor(parts, y * X + lax.axis_index("xx"))
    table_sum = sum(parts[1:], parts[0])
    tables = [table_sum] + [shift(table_sum, "hz", d) for d in range(1, Z)]
    table_total = jnp.concatenate(from_cyclic(tables, z), axis=0).T

    shard_second = line_reduce(grad_out_blocks)
    first_sum = line_reduce(grad_in_blocks).reshape(Y, D // N, FF // Y)
    first_low = first_sum.astype(LOW)
    first_parts = [pick(first_sum, y)] + [
        swap(pick(first_low, y ^ k), ("yy",), k).astype(WIDE) for k in range(1, Y)
    ]
    first_parts = jnp.stack(from_xor(first_parts, y))
    shard_first = (
        first_parts.reshape(Y, D // N, Z, part_ff).transpose(1, 2, 0, 3).reshape(D // N, FF)
    )
    return (
        output[None],
        grad_inputs[None],
        shard_gain_one,
        shard_qkv,
        shard_attn_out,
        table_total,
        shard_gain_two,
        shard_router,
        shard_first[None],
        shard_second[None],
    )


def solution(mesh):
    devices_ctx, devices_exp = mesh.shape["ctx"], mesh.shape["exp"]
    outer = 4
    parts = Mesh(
        mesh.devices.reshape(outer, devices_ctx // outer, devices_exp // 2, 2),
        ("hz", "yy", "xx", "cc"),
    )
    ctx, exp = ("hz", "yy"), ("xx", "cc")
    every = ctx + exp
    tokens = P(exp, ctx, None)
    return jax.shard_map(
        body,
        mesh=parts,
        in_specs=(
            tokens,
            P(every),
            P(every, None),
            P(every, None),
            P(),
            P(every),
            P(every, None),
            tokens,
            tokens,
            tokens,
            P(),
            tokens,
        ),
        out_specs=(
            tokens,
            tokens,
            P(every),
            P(every, None),
            P(every, None),
            P(),
            P(every),
            P(every, None),
            tokens,
            tokens,
        ),
        check_vma=False,
    )
```

```python
import jax
import jax.numpy as jnp
from jax import lax
from jax.experimental import pallas as pl
from jax.experimental.pallas import tpu as pltpu
from jax.sharding import Mesh, PartitionSpec as P

PRECISION_FULL = lax.Precision.HIGHEST
MASKED = -1e30
LOW = jnp.bfloat16
WIDE = jnp.float32
EPS = 1e-06
LAYER = ("yy", "xx", "cc")


def dot(left, right, contract):
    return lax.dot_general(left, right, (contract, ((), ())), preferred_element_type=WIDE)


def shift(x, axis, d):
    n = lax.axis_size(axis)
    return lax.ppermute(x, axis, [((j + d) % n, j) for j in range(n)])


def swap(x, axes, k):
    n = 1
    for axis in axes:
        n *= lax.axis_size(axis)
    return lax.ppermute(x, axes, [(j ^ k, j) for j in range(n)])


def from_xor(blocks, me):
    step = 1
    while step < len(blocks):
        flip = (me & step) != 0
        blocks = [jnp.where(flip, blocks[j ^ step], blocks[j]) for j in range(len(blocks))]
        step *= 2
    return blocks


def from_cyclic(blocks, me):
    n, step = len(blocks), 1
    while step < n:
        move = (me & step) != 0
        blocks = [jnp.where(move, blocks[(j - step) % n], blocks[j]) for j in range(n)]
        step *= 2
    return blocks


def after(x, *others):
    for other in others:
        first = lax.slice(other, (0,) * other.ndim, (1,) * other.ndim).reshape(())
        x = x + (first * 0).astype(x.dtype)
    return x


def expert_kernel(both, w_first, w_second, out, grad_first, grad_second, total, rows_t):
    step, steps = pl.program_id(0), pl.num_programs(0)
    width = w_first.shape[0]
    rows, grads = both[:, :width], both[:, width:]

    @pl.when(step == 0)
    def _():
        rows_t[...] = rows.T
        total[...] = jnp.zeros_like(total)

    hidden = dot(rows, w_first[...], ((1,), (0,)))
    square = hidden * hidden
    curve = jnp.tanh(0.7978845608028654 * (hidden + 0.044715 * square * hidden))
    active = (0.5 * hidden * (1.0 + curve)).astype(LOW)
    slope = 0.5 * (1.0 + curve) + 0.5 * hidden * (1.0 - curve * curve) * (
        0.7978845608028654 * (1.0 + 0.134145 * square)
    )
    total[:, :width] += dot(active, w_second[...], ((1,), (0,)))
    grad_second[...] = dot(active, grads, ((0,), (0,))).astype(LOW)
    grad_active = dot(grads, w_second[...], ((1,), (1,)))
    grad_hidden = (slope * grad_active).astype(LOW)
    total[:, width:] += dot(grad_hidden, w_first[...], ((1,), (1,)))
    grad_first[...] = dot(rows_t[...], grad_hidden, ((1,), (0,))).astype(LOW)

    @pl.when(step == steps - 1)
    def _():
        out[...] = total[...].astype(LOW)


def expert(both, w_first, w_second, block):
    count, width, units = both.shape[0], w_first.shape[0], w_first.shape[1]
    whole = pl.BlockSpec(memory_space=pltpu.VMEM)
    flops = 12 * count * width * units
    return pl.pallas_call(
        expert_kernel,
        grid=(units // block,),
        out_shape=(
            jax.ShapeDtypeStruct(both.shape, LOW),
            jax.ShapeDtypeStruct(w_first.shape, LOW),
            jax.ShapeDtypeStruct(w_second.shape, LOW),
        ),
        in_specs=[
            whole,
            pl.BlockSpec((width, block), lambda i: (0, i)),
            pl.BlockSpec((block, width), lambda i: (i, 0)),
        ],
        out_specs=(
            whole,
            pl.BlockSpec((width, block), lambda i: (0, i)),
            pl.BlockSpec((block, width), lambda i: (i, 0)),
        ),
        scratch_shapes=[pltpu.VMEM(both.shape, WIDE), pltpu.VMEM((width, count), LOW)],
        compiler_params=pltpu.CompilerParams(vmem_limit_bytes=56 * 1024 * 1024),
        cost_estimate=pl.CostEstimate(
            flops=flops, bytes_accessed=4 * both.size + 8 * w_first.size, transcendentals=count * units
        ),
    )(both, w_first, w_second)


def pick(stack, index):
    return lax.dynamic_index_in_dim(stack, index, 0, keepdims=False)


def layer_gather(block):
    yx_count = lax.axis_size("yy") * lax.axis_size("xx")
    me_yx = lax.axis_index("yy") * lax.axis_size("xx") + lax.axis_index("xx")
    blocks = [block] + [swap(block, ("yy", "xx"), k) for k in range(1, yx_count)]
    joined = jnp.stack(from_xor(blocks, me_yx))
    both = from_xor([joined, swap(joined, ("cc",), 1)], lax.axis_index("cc"))
    full = jnp.stack(both)
    cores, layers, outer, rows, width = full.shape
    return full.transpose(2, 1, 0, 3, 4).reshape(outer * layers * cores * rows, width)


def every_block(x, axes):
    return lax.all_to_all(x, axes, split_axis=0, concat_axis=0, tiled=True)


def low_terms(x):
    return jnp.concatenate(three_terms(x), axis=0)


def three_terms(x):
    high = lax.reduce_precision(x, 8, 7)
    rest = x - high
    middle = lax.reduce_precision(rest, 8, 7)
    return high.astype(LOW), middle.astype(LOW), (rest - middle).astype(LOW)


def body(
    activations,
    gain_one,
    query_key_value_weight,
    attention_output_weight,
    pos_table,
    gain_two,
    w_router,
    w_in,
    w_out,
    routes,
    pair_of_device,
    cotangent,
):
    Z, Y = lax.axis_size("hz"), lax.axis_size("yy")
    E, N = lax.axis_size("xx") * lax.axis_size("cc"), Z * Y
    z, y = lax.axis_index("hz"), lax.axis_index("yy")
    _, own_rows, D = activations.shape
    half = own_rows // 2
    buckets, heads = pos_table.shape
    hd = D // heads
    hg = heads // Z
    gw = hg * hd
    top = routes.shape[2]
    shard = gain_one.shape[0]
    FF = w_in.shape[2]
    capacity = max(2, 5 * own_rows * top // (4 * E))

    acts = activations[0]
    act_blocks = [acts] + [shift(acts, "hz", d) for d in range(1, Z)]
    small = jnp.concatenate([gain_one[:, None], gain_two[:, None], w_router], axis=1)
    small_width = -(-(gw + small.shape[1]) // 128) * 128 - gw
    small = jnp.pad(small, ((0, 0), (0, small_width - small.shape[1])))

    def qkv_piece(group):
        columns = [
            lax.dynamic_slice(query_key_value_weight, (0, part * D + group * gw), (shard, gw))
            for part in (1, 2, 0)
        ]
        return jnp.concatenate(columns + [small], axis=1)

    pieces = [qkv_piece(z)] + [shift(qkv_piece((z - d) % Z), "hz", d) for d in range(1, Z)]
    w_all = layer_gather(jnp.stack(from_cyclic(pieces, z)))

    w_second = lax.all_gather(w_out[0], "hz", axis=0, tiled=True)
    part_ff = FF // N

    def in_piece(part):
        columns = [
            lax.dynamic_slice(w_in[0], (0, (g * Y + part) * part_ff), (D // N, part_ff))
            for g in range(Z)
        ]
        return jnp.concatenate(columns, axis=1)

    in_rows = [in_piece(y)] + [
        swap(after(in_piece(y ^ k), *pieces[1:]), ("yy",), k) for k in range(1, Y)
    ]
    in_rows = jnp.concatenate(from_xor(in_rows, y), axis=0)
    w_first = lax.all_gather(in_rows, "hz", axis=0, tiled=True)

    own_attn_w = after(attention_output_weight, w_all)
    attn_w_pieces = [own_attn_w] + [shift(own_attn_w, "hz", d) for d in range(1, Z)]
    w_attn_out = layer_gather(jnp.stack(from_cyclic(attn_w_pieces, z)))

    gain_first = w_all[:, 3 * gw].astype(WIDE)
    gain_second = w_all[:, 3 * gw + 1].astype(WIDE)
    router = w_all[:, 3 * gw + 2 : 3 * gw + 2 + E]

    n_q, n_k = 2 * Z, 2 * Z * Y

    def tile_of(count, width, axis):
        shape = (count, 1) if axis == 0 else (1, count)
        entry = lax.broadcasted_iota(jnp.int32, shape, axis) // width
        owner = ((z + (entry // 2) % Z) % Z) * Y + (y ^ (entry // (2 * Z)))
        hot_shape = (count, N) if axis == 0 else (N, count)
        lanes = lax.broadcasted_iota(jnp.int32, hot_shape, 1 - axis)
        pairs = pair_of_device[None, :] if axis == 0 else pair_of_device[:, None]
        first = jnp.sum(jnp.where(lanes == owner, pairs, 0), axis=1 - axis, keepdims=True)
        return jnp.where(entry % 2 == 0, first, 2 * N - 1 - first)

    def position_of(count, axis):
        shape = (count, 1) if axis == 0 else (1, count)
        within = lax.broadcasted_iota(jnp.int32, shape, axis) % half
        return tile_of(count, half, axis) * half + within

    query_pos = position_of(n_q * half, 0)
    key_pos = position_of(n_k * half, 1)
    bucket = jnp.clip(tile_of(n_q, 1, 0) - tile_of(n_k, 1, 1), 0, buckets - 1)
    levels = lax.broadcasted_iota(jnp.int32, (n_q, n_k, buckets), 2)
    bucket_hot = bucket[:, :, None] == levels
    own_table = lax.dynamic_slice(pos_table, (0, z * hg), (buckets, hg)).T
    tile_bias = jnp.sum(jnp.where(bucket_hot[None], own_table[:, None, None, :], 0.0), axis=-1)
    bias_terms = jnp.concatenate(three_terms(tile_bias), axis=-1)
    bias_rows = jnp.broadcast_to(
        bias_terms[:, :, None, :], (hg, n_q, half, 3 * n_k)
    ).reshape(hg, n_q * half, 3 * n_k)
    key_hot = (
        lax.broadcasted_iota(jnp.int32, (n_k * half, n_k), 0) // half
        == lax.broadcasted_iota(jnp.int32, (n_k * half, n_k), 1)
    ).astype(LOW)

    x_rows = jnp.concatenate(act_blocks, axis=0).astype(WIDE)
    scale_one = lax.rsqrt(jnp.mean(x_rows * x_rows, axis=-1, keepdims=True) + EPS)
    hat_one = x_rows * scale_one
    normed_one = (hat_one * gain_first).astype(LOW)
    w_kv, w_q = w_all[:, : 2 * gw], w_all[:, 2 * gw : 3 * gw]
    kv = dot(normed_one, w_kv, ((1,), (0,))).astype(LOW)
    kv_all = jnp.concatenate([kv] + [swap(kv, ("yy",), k) for k in range(1, Y)], axis=0)
    q = dot(normed_one, w_q, ((1,), (0,))).astype(LOW)

    def by_head(rows):
        return rows.reshape(rows.shape[0], hg, hd).transpose(1, 0, 2)

    q_heads = by_head(q) * jnp.asarray(hd**-0.5, LOW)
    k_heads, v_heads = by_head(kv_all[:, :gw]), by_head(kv_all[:, gw:])
    q_wide = jnp.concatenate([q_heads, bias_rows], axis=-1)
    k_hot = jnp.broadcast_to(key_hot[None], (hg,) + key_hot.shape)
    k_wide = jnp.concatenate([k_heads, k_hot, k_hot, k_hot], axis=-1)
    scores = jnp.einsum("hqe,hke->hqk", q_wide, k_wide, preferred_element_type=WIDE)
    visible = query_pos >= key_pos
    scores = jnp.where(visible[None], scores, MASKED)
    weights = jnp.exp(scores - jnp.max(scores, axis=-1, keepdims=True))
    probs = weights / jnp.sum(weights, axis=-1, keepdims=True)
    probs_low = probs.astype(LOW)
    mixed_heads = jnp.einsum("hqk,hke->qhe", probs_low, v_heads, preferred_element_type=WIDE)
    mixed = mixed_heads.reshape(Z, own_rows, gw).astype(LOW)
    mixed_back = [mixed[0]] + [shift(mixed[d], "hz", -d) for d in range(1, Z)]
    mixed_back = from_cyclic([mixed_back[-d % Z] for d in range(Z)], z)
    mixed_full = jnp.concatenate(mixed_back, axis=-1)

    own_x = acts.astype(WIDE)
    resid = own_x + dot(mixed_full, w_attn_out, ((1,), (0,)))
    scale_two = lax.rsqrt(jnp.mean(resid * resid, axis=-1, keepdims=True) + EPS)
    hat_two = resid * scale_two
    normed_two = (hat_two * gain_second).astype(LOW)

    choices = [routes[0][:, t : t + 1] for t in range(top)]
    expert_iota = lax.broadcasted_iota(jnp.int32, (1, E), 1)
    chosen_masks = [(choice == expert_iota).astype(WIDE) for choice in choices]
    flat = jnp.concatenate(choices, axis=0)
    hits = (flat == expert_iota).astype(LOW)
    pairs = (own_rows * top, own_rows * top)
    earlier = lax.broadcasted_iota(jnp.int32, pairs, 0) > lax.broadcasted_iota(jnp.int32, pairs, 1)
    before = dot(earlier.astype(LOW), hits, ((1,), (0,)))
    rank = jnp.sum(before * hits.astype(WIDE), axis=-1, keepdims=True).astype(jnp.int32)
    target = flat * capacity + rank
    slots = E * capacity
    slot_iota = lax.broadcasted_iota(jnp.int32, (1, Y * slots), 1) % slots
    route_map = (target == slot_iota).astype(LOW)
    maps = [route_map[t * own_rows : (t + 1) * own_rows] for t in range(top)]
    per_token = sum(maps[1:], maps[0])

    def exchange(rows):
        blocks = rows.reshape(Y * E, capacity, rows.shape[1])
        return every_block(blocks, LAYER).reshape(rows.shape)

    rows = dot(per_token, normed_two, ((0,), (0,)))
    router_logits = dot(normed_two, router, ((1,), (0,)))
    chosen = [jnp.sum(mask * router_logits, axis=-1, keepdims=True) for mask in chosen_masks]
    highest = chosen[0]
    for value in chosen[1:]:
        highest = jnp.maximum(highest, value)
    raised = [jnp.exp(value - highest) for value in chosen]
    gates = [value / sum(raised[1:], raised[0]) for value in raised]
    cot = cotangent[0]
    grad_picked = jnp.concatenate([(gate * cot).astype(LOW) for gate in gates], axis=0)
    grad_rows = dot(route_map, grad_picked, ((0,), (0,)))
    both = exchange(jnp.concatenate([rows, grad_rows], axis=1).astype(LOW))

    block = part_ff if part_ff % 128 == 0 else FF // Y
    results, grad_first, grad_second = expert(both, w_first, w_second, block)
    back = exchange(results)
    returned, coming = back[:, :D], back[:, D:]
    first_low = lax.psum_scatter(grad_first, "hz", scatter_dimension=0, tiled=True)
    shard_second = lax.psum_scatter(grad_second, "hz", scatter_dimension=0, tiled=True)

    picked = [dot(one, returned, ((1,), (0,))) for one in maps]
    output = resid
    for gate, rows_of in zip(gates, picked):
        output = output + gate * rows_of
    grad_gates = [jnp.sum(rows_of * cot, axis=-1, keepdims=True) for rows_of in picked]
    inner = sum(gate * grad for gate, grad in zip(gates, grad_gates))
    logit_gradient = sum(
        gate * (grad - inner) * mask
        for gate, grad, mask in zip(gates, grad_gates, chosen_masks)
    )
    grad_normed_two = dot(per_token, coming, ((1,), (0,))) + jnp.einsum(
        "te,de->td", logit_gradient, router.astype(WIDE), precision=PRECISION_FULL
    )
    grad_router = jnp.einsum(
        "td,te->de", normed_two.astype(WIDE), logit_gradient, precision=PRECISION_FULL
    )
    grad_gain_two = jnp.sum(grad_normed_two * hat_two, axis=0)
    grad_hat = grad_normed_two * gain_second
    grad_resid = cot + scale_two * (
        grad_hat - hat_two * jnp.mean(grad_hat * hat_two, axis=-1, keepdims=True)
    )
    grad_attention = grad_resid.astype(LOW)
    grad_attn_out = dot(mixed_full, grad_attention, ((0,), (0,)))
    grad_mixed = lax.dot_general(
        w_attn_out.reshape(Z, gw, D),
        grad_attention,
        (((2,), (1,)), ((), ())),
        preferred_element_type=WIDE,
    ).transpose(0, 2, 1).astype(LOW)
    grad_mixed_rows = jnp.concatenate(
        [pick(grad_mixed, z)]
        + [shift(pick(grad_mixed, (z - d) % Z), "hz", d) for d in range(1, Z)],
        axis=0,
    )

    grad_heads = by_head(grad_mixed_rows)
    row_dot = jnp.sum(
        by_head(mixed.reshape(Z * own_rows, gw)).astype(WIDE) * grad_heads.astype(WIDE),
        axis=-1,
        keepdims=True,
    )
    grad_probs = jnp.einsum("hqe,hke->hqk", grad_heads, v_heads, preferred_element_type=WIDE)
    grad_scores = (probs_low.astype(WIDE) * (grad_probs - row_dot)).astype(LOW)
    grad_q_wide = jnp.einsum(
        "hqk,hke->hqe",
        grad_scores,
        jnp.concatenate([k_heads, k_hot], axis=-1),
        preferred_element_type=WIDE,
    )
    grad_q = grad_q_wide[..., :hd] * hd**-0.5
    tile_sums = grad_q_wide[..., hd:].reshape(hg, n_q, half, n_k).sum(axis=2)
    table_part = jnp.sum(
        jnp.where(bucket_hot[None], tile_sums[..., None], 0.0), axis=(1, 2)
    )
    grad_k = jnp.einsum("hqk,hqe->khe", grad_scores, q_heads, preferred_element_type=WIDE)
    grad_v = jnp.einsum("hqk,hqe->khe", probs_low, grad_heads, preferred_element_type=WIDE)
    grad_kv = jnp.concatenate(
        [grad_k.reshape(-1, gw), grad_v.reshape(-1, gw)], axis=1
    ).reshape(Y, Z * own_rows, 2 * gw)
    grad_kv_own = grad_kv[0]
    for k in range(1, Y):
        grad_kv_own = grad_kv_own + swap(grad_kv[k].astype(LOW), ("yy",), k).astype(WIDE)
    grad_q_rows = grad_q.transpose(1, 0, 2).reshape(-1, gw)
    grad_qkv = jnp.concatenate([grad_kv_own, grad_q_rows], axis=1).astype(LOW)

    grad_normed_part = dot(grad_qkv, w_all[:, : 3 * gw], ((1,), (1,)))
    grad_gain_one = jnp.sum(grad_normed_part * hat_one, axis=0)
    grad_low = grad_normed_part.astype(LOW).reshape(Z, own_rows, D)
    grad_normed_one = grad_normed_part[:own_rows]
    for d in range(1, Z):
        grad_normed_one = grad_normed_one + shift(grad_low[d], "hz", -d).astype(WIDE)
    own_hat = hat_one[:own_rows]
    grad_hat_one = grad_normed_one * gain_first
    grad_inputs = grad_resid + scale_one[:own_rows] * (
        grad_hat_one - own_hat * jnp.mean(grad_hat_one * own_hat, axis=-1, keepdims=True)
    )

    def pad_columns(columns):
        return jnp.pad(columns, ((0, 0), (0, 128 - columns.shape[1])))

    attn_part = jnp.concatenate(
        [grad_attn_out, pad_columns(jnp.concatenate([grad_gain_two[:, None], grad_router], 1))],
        axis=1,
    )
    attn_part = attn_part.astype(LOW)
    attn_width = attn_part.shape[1]
    line_rows = Z * shard
    table_size = 3 * hg * buckets

    def table_columns(table, rows):
        width = -(-table_size // rows)
        terms = jnp.pad(low_terms(table).reshape(-1), (0, rows * width - table_size))
        return terms.reshape(rows, width)

    def table_of(columns):
        terms = columns.reshape(columns.shape[0], -1)[:, :table_size]
        return terms.reshape(-1, 3, hg, buckets).sum(axis=1)

    grad_w_qkv = dot(normed_one, grad_qkv, ((0,), (0,))).astype(LOW)
    table_block = table_columns(table_part, line_rows)
    table_width = table_block.shape[1]
    extra = jnp.concatenate(
        [
            grad_gain_one[:, None].astype(LOW).reshape(Z, -1, shard, 1),
            jnp.broadcast_to(
                table_block.reshape(Z, 1, shard, table_width),
                (Z, Y * E, shard, table_width),
            ),
        ],
        axis=3,
    ).reshape(D, 1 + table_width)
    extra_width = -(-(3 * gw + 1 + table_width) // 128) * 128 - 3 * gw
    extra = jnp.pad(extra, ((0, 0), (0, extra_width - 1 - table_width)))
    outer_blocks = jnp.concatenate([grad_w_qkv, extra, attn_part], axis=1)
    full_width = outer_blocks.shape[1]
    outer_blocks = outer_blocks.reshape(Z, Y * E, shard, full_width).transpose(1, 0, 2, 3)
    got = every_block(outer_blocks.reshape(Y * E, line_rows, full_width), LAYER)
    got = got.astype(WIDE)
    layer_sum = got.sum(axis=0)
    qkv_sum, attn_sum = layer_sum[:, : 3 * gw + 1], layer_sum[:, full_width - attn_width :]
    layer_table = table_of(got[:, :, 3 * gw + 1 : 3 * gw + 1 + table_width]).sum(axis=0)
    table_block = table_columns(layer_table, shard)
    line_width = table_block.shape[1]
    line_blocks = jnp.concatenate(
        [
            attn_sum.astype(LOW).reshape(Z, shard, attn_width),
            qkv_sum.astype(LOW).reshape(Z, shard, 3 * gw + 1),
            jnp.broadcast_to(table_block[None], (Z, shard, line_width)),
        ],
        axis=2,
    )
    line_pad = -(-line_blocks.shape[2] // 128) * 128 - line_blocks.shape[2]
    line_blocks = jnp.pad(line_blocks, ((0, 0), (0, 0), (0, line_pad)))
    line = every_block(line_blocks, ("hz",)).astype(WIDE)
    attn_total, line = line[:, :, :attn_width].sum(axis=0), line[:, :, attn_width:]
    shard_attn_out = attn_total[:, :D]
    shard_gain_two = attn_total[:, D]
    shard_router = attn_total[:, D + 1 : D + 1 + E]
    shard_gain_one = line[:, :, 3 * gw].sum(axis=0)
    shard_qkv = jnp.concatenate(
        [line[g, :, part * gw : (part + 1) * gw] for part in (2, 0, 1) for g in range(Z)], axis=1
    )
    tables = table_of(line[:, :, 3 * gw + 1 : 3 * gw + 1 + line_width])
    table_total = tables.reshape(heads, buckets).T

    shard_second = shard_second.astype(WIDE)
    first_low = first_low.reshape(Y, D // N, FF // Y)
    first_parts = [pick(first_low, y)] + [
        swap(pick(first_low, y ^ k), ("yy",), k) for k in range(1, Y)
    ]
    first_parts = from_xor(first_parts, y)
    shard_first = jnp.concatenate(
        [
            first_parts[k][:, g * part_ff : (g + 1) * part_ff]
            for g in range(Z)
            for k in range(Y)
        ],
        axis=1,
    ).astype(WIDE)
    return (
        output[None],
        grad_inputs[None],
        shard_gain_one,
        shard_qkv,
        shard_attn_out,
        table_total,
        shard_gain_two,
        shard_router,
        shard_first[None],
        shard_second[None],
    )


def solution(mesh):
    devices_ctx, devices_exp = mesh.shape["ctx"], mesh.shape["exp"]
    outer = 4
    parts = Mesh(
        mesh.devices.reshape(outer, devices_ctx // outer, devices_exp // 2, 2),
        ("hz", "yy", "xx", "cc"),
    )
    ctx, exp = ("hz", "yy"), ("xx", "cc")
    every = ctx + exp
    tokens = P(exp, ctx, None)
    return jax.shard_map(
        body,
        mesh=parts,
        in_specs=(
            tokens,
            P(every),
            P(every, None),
            P(every, None),
            P(),
            P(every),
            P(every, None),
            tokens,
            tokens,
            tokens,
            P(),
            tokens,
        ),
        out_specs=(
            tokens,
            tokens,
            P(every),
            P(every, None),
            P(every, None),
            P(),
            P(every),
            P(every, None),
            tokens,
            tokens,
        ),
        check_vma=False,
    )
```

```python
import jax
import jax.numpy as jnp
from jax import lax
from jax.experimental import pallas as pl
from jax.experimental.pallas import tpu as pltpu
from jax.sharding import Mesh, PartitionSpec as P

PRECISION_FULL = lax.Precision.HIGHEST
MASKED = -1e30
LOW = jnp.bfloat16
WIDE = jnp.float32
EPS = 1e-06
LAYER = ("yy", "xx", "cc")


def dot(left, right, contract):
    return lax.dot_general(left, right, (contract, ((), ())), preferred_element_type=WIDE)


def shift(x, axis, d):
    n = lax.axis_size(axis)
    return lax.ppermute(x, axis, [((j + d) % n, j) for j in range(n)])


def swap(x, axes, k):
    n = 1
    for axis in axes:
        n *= lax.axis_size(axis)
    return lax.ppermute(x, axes, [(j ^ k, j) for j in range(n)])


def from_xor(blocks, me):
    step = 1
    while step < len(blocks):
        flip = (me & step) != 0
        blocks = [jnp.where(flip, blocks[j ^ step], blocks[j]) for j in range(len(blocks))]
        step *= 2
    return blocks


def from_cyclic(blocks, me):
    n, step = len(blocks), 1
    while step < n:
        move = (me & step) != 0
        blocks = [jnp.where(move, blocks[(j - step) % n], blocks[j]) for j in range(n)]
        step *= 2
    return blocks


def after(x, *others):
    for other in others:
        first = lax.slice(other, (0,) * other.ndim, (1,) * other.ndim).reshape(())
        x = x + (first * 0).astype(x.dtype)
    return x


def expert_kernel(both, w_first, w_second, out, grad_first, grad_second, total, rows_t):
    step, steps = pl.program_id(0), pl.num_programs(0)
    width = w_first.shape[0]
    rows, grads = both[:, :width], both[:, width:]

    @pl.when(step == 0)
    def _():
        rows_t[...] = rows.T
        total[...] = jnp.zeros_like(total)

    hidden = dot(rows, w_first[...], ((1,), (0,)))
    square = hidden * hidden
    curve = jnp.tanh(0.7978845608028654 * (hidden + 0.044715 * square * hidden))
    active = (0.5 * hidden * (1.0 + curve)).astype(LOW)
    slope = 0.5 * (1.0 + curve) + 0.5 * hidden * (1.0 - curve * curve) * (
        0.7978845608028654 * (1.0 + 0.134145 * square)
    )
    total[:, :width] += dot(active, w_second[...], ((1,), (0,)))
    grad_second[...] = dot(active, grads, ((0,), (0,))).astype(LOW)
    grad_active = dot(grads, w_second[...], ((1,), (1,)))
    grad_hidden = (slope * grad_active).astype(LOW)
    total[:, width:] += dot(grad_hidden, w_first[...], ((1,), (1,)))
    grad_first[...] = dot(rows_t[...], grad_hidden, ((1,), (0,))).astype(LOW)

    @pl.when(step == steps - 1)
    def _():
        out[...] = total[...].astype(LOW)


def expert(both, w_first, w_second, block):
    count, width, units = both.shape[0], w_first.shape[0], w_first.shape[1]
    whole = pl.BlockSpec(memory_space=pltpu.VMEM)
    flops = 12 * count * width * units
    return pl.pallas_call(
        expert_kernel,
        grid=(units // block,),
        out_shape=(
            jax.ShapeDtypeStruct(both.shape, LOW),
            jax.ShapeDtypeStruct(w_first.shape, LOW),
            jax.ShapeDtypeStruct(w_second.shape, LOW),
        ),
        in_specs=[
            whole,
            pl.BlockSpec((width, block), lambda i: (0, i)),
            pl.BlockSpec((block, width), lambda i: (i, 0)),
        ],
        out_specs=(
            whole,
            pl.BlockSpec((width, block), lambda i: (0, i)),
            pl.BlockSpec((block, width), lambda i: (i, 0)),
        ),
        scratch_shapes=[pltpu.VMEM(both.shape, WIDE), pltpu.VMEM((width, count), LOW)],
        compiler_params=pltpu.CompilerParams(vmem_limit_bytes=56 * 1024 * 1024),
        cost_estimate=pl.CostEstimate(
            flops=flops, bytes_accessed=4 * both.size + 8 * w_first.size, transcendentals=count * units
        ),
    )(both, w_first, w_second)


def pick(stack, index):
    return lax.dynamic_index_in_dim(stack, index, 0, keepdims=False)


def layer_gather(block):
    yx_count = lax.axis_size("yy") * lax.axis_size("xx")
    me_yx = lax.axis_index("yy") * lax.axis_size("xx") + lax.axis_index("xx")
    blocks = [block] + [swap(block, ("yy", "xx"), k) for k in range(1, yx_count)]
    joined = jnp.stack(from_xor(blocks, me_yx))
    both = from_xor([joined, swap(joined, ("cc",), 1)], lax.axis_index("cc"))
    full = jnp.stack(both)
    cores, layers, outer, rows, width = full.shape
    return full.transpose(2, 1, 0, 3, 4).reshape(outer * layers * cores * rows, width)


def every_block(x, axes):
    return lax.all_to_all(x, axes, split_axis=0, concat_axis=0, tiled=True)


def low_terms(x):
    return jnp.concatenate(three_terms(x), axis=0)


def three_terms(x):
    high = lax.reduce_precision(x, 8, 7)
    rest = x - high
    middle = lax.reduce_precision(rest, 8, 7)
    return high.astype(LOW), middle.astype(LOW), (rest - middle).astype(LOW)


def body(
    activations,
    gain_one,
    query_key_value_weight,
    attention_output_weight,
    pos_table,
    gain_two,
    w_router,
    w_in,
    w_out,
    routes,
    pair_of_device,
    cotangent,
):
    Z, Y = lax.axis_size("hz"), lax.axis_size("yy")
    E, N = lax.axis_size("xx") * lax.axis_size("cc"), Z * Y
    z, y = lax.axis_index("hz"), lax.axis_index("yy")
    _, own_rows, D = activations.shape
    half = own_rows // 2
    buckets, heads = pos_table.shape
    hd = D // heads
    hg = heads // Z
    gw = hg * hd
    top = routes.shape[2]
    shard = gain_one.shape[0]
    FF = w_in.shape[2]
    capacity = max(2, 5 * own_rows * top // (4 * E))

    acts = activations[0]
    act_blocks = [acts] + [shift(acts, "hz", d) for d in range(1, Z)]
    small = jnp.concatenate([gain_one[:, None], gain_two[:, None], w_router], axis=1)
    small_width = -(-(gw + small.shape[1]) // 128) * 128 - gw
    small = jnp.pad(small, ((0, 0), (0, small_width - small.shape[1])))

    def qkv_piece(group):
        columns = [
            lax.dynamic_slice(query_key_value_weight, (0, part * D + group * gw), (shard, gw))
            for part in (1, 2, 0)
        ]
        return jnp.concatenate(columns + [small], axis=1)

    pieces = [qkv_piece(z)] + [shift(qkv_piece((z - d) % Z), "hz", d) for d in range(1, Z)]
    w_all = layer_gather(jnp.stack(from_cyclic(pieces, z)))

    w_second = lax.all_gather(w_out[0], "hz", axis=0, tiled=True)
    part_ff = FF // N

    def in_piece(part):
        columns = [
            lax.dynamic_slice(w_in[0], (0, (g * Y + part) * part_ff), (D // N, part_ff))
            for g in range(Z)
        ]
        return jnp.concatenate(columns, axis=1)

    in_rows = [in_piece(y)] + [
        swap(after(in_piece(y ^ k), *pieces[1:]), ("yy",), k) for k in range(1, Y)
    ]
    in_rows = jnp.concatenate(from_xor(in_rows, y), axis=0)
    w_first = lax.all_gather(in_rows, "hz", axis=0, tiled=True)

    own_attn_w = after(attention_output_weight, w_all)
    attn_w_pieces = [own_attn_w] + [shift(own_attn_w, "hz", d) for d in range(1, Z)]
    w_attn_out = layer_gather(jnp.stack(from_cyclic(attn_w_pieces, z)))

    gain_first = w_all[:, 3 * gw].astype(WIDE)
    gain_second = w_all[:, 3 * gw + 1].astype(WIDE)
    router = w_all[:, 3 * gw + 2 : 3 * gw + 2 + E]

    n_q, n_k = 2 * Z, 2 * Z * Y

    def tile_of(count, width, axis):
        shape = (count, 1) if axis == 0 else (1, count)
        entry = lax.broadcasted_iota(jnp.int32, shape, axis) // width
        owner = ((z + (entry // 2) % Z) % Z) * Y + (y ^ (entry // (2 * Z)))
        hot_shape = (count, N) if axis == 0 else (N, count)
        lanes = lax.broadcasted_iota(jnp.int32, hot_shape, 1 - axis)
        pairs = pair_of_device[None, :] if axis == 0 else pair_of_device[:, None]
        first = jnp.sum(jnp.where(lanes == owner, pairs, 0), axis=1 - axis, keepdims=True)
        return jnp.where(entry % 2 == 0, first, 2 * N - 1 - first)

    def position_of(count, axis):
        shape = (count, 1) if axis == 0 else (1, count)
        within = lax.broadcasted_iota(jnp.int32, shape, axis) % half
        return tile_of(count, half, axis) * half + within

    query_pos = position_of(n_q * half, 0)
    key_pos = position_of(n_k * half, 1)
    bucket = jnp.clip(tile_of(n_q, 1, 0) - tile_of(n_k, 1, 1), 0, buckets - 1)
    levels = lax.broadcasted_iota(jnp.int32, (n_q, n_k, buckets), 2)
    bucket_hot = bucket[:, :, None] == levels
    own_table = lax.dynamic_slice(pos_table, (0, z * hg), (buckets, hg)).T
    tile_bias = jnp.sum(jnp.where(bucket_hot[None], own_table[:, None, None, :], 0.0), axis=-1)
    bias_terms = jnp.concatenate(three_terms(tile_bias), axis=-1)
    bias_rows = jnp.broadcast_to(
        bias_terms[:, :, None, :], (hg, n_q, half, 3 * n_k)
    ).reshape(hg, n_q * half, 3 * n_k)
    key_hot = (
        lax.broadcasted_iota(jnp.int32, (n_k * half, n_k), 0) // half
        == lax.broadcasted_iota(jnp.int32, (n_k * half, n_k), 1)
    ).astype(LOW)

    x_rows = jnp.concatenate(act_blocks, axis=0).astype(WIDE)
    scale_one = lax.rsqrt(jnp.mean(x_rows * x_rows, axis=-1, keepdims=True) + EPS)
    hat_one = x_rows * scale_one
    normed_one = (hat_one * gain_first).astype(LOW)
    w_kv, w_q = w_all[:, : 2 * gw], w_all[:, 2 * gw : 3 * gw]
    kv = dot(normed_one, w_kv, ((1,), (0,))).astype(LOW)
    kv_all = jnp.concatenate([kv] + [swap(kv, ("yy",), k) for k in range(1, Y)], axis=0)
    q = dot(normed_one, w_q, ((1,), (0,))).astype(LOW)

    def by_head(rows):
        return rows.reshape(rows.shape[0], hg, hd).transpose(1, 0, 2)

    q_heads = by_head(q) * jnp.asarray(hd**-0.5, LOW)
    k_heads, v_heads = by_head(kv_all[:, :gw]), by_head(kv_all[:, gw:])
    q_wide = jnp.concatenate([q_heads, bias_rows], axis=-1)
    k_hot = jnp.broadcast_to(key_hot[None], (hg,) + key_hot.shape)
    k_wide = jnp.concatenate([k_heads, k_hot, k_hot, k_hot], axis=-1)
    scores = jnp.einsum("hqe,hke->hqk", q_wide, k_wide, preferred_element_type=WIDE)
    visible = query_pos >= key_pos
    scores = jnp.where(visible[None], scores, MASKED)
    weights = jnp.exp(scores - jnp.max(scores, axis=-1, keepdims=True))
    probs = weights / jnp.sum(weights, axis=-1, keepdims=True)
    probs_low = probs.astype(LOW)
    mixed_heads = jnp.einsum("hqk,hke->qhe", probs_low, v_heads, preferred_element_type=WIDE)
    mixed = mixed_heads.reshape(Z, own_rows, gw).astype(LOW)
    mixed_back = [mixed[0]] + [shift(mixed[d], "hz", -d) for d in range(1, Z)]
    mixed_back = from_cyclic([mixed_back[-d % Z] for d in range(Z)], z)
    mixed_full = jnp.concatenate(mixed_back, axis=-1)

    own_x = acts.astype(WIDE)
    resid = own_x + dot(mixed_full, w_attn_out, ((1,), (0,)))
    scale_two = lax.rsqrt(jnp.mean(resid * resid, axis=-1, keepdims=True) + EPS)
    hat_two = resid * scale_two
    normed_two = (hat_two * gain_second).astype(LOW)

    choices = [routes[0][:, t : t + 1] for t in range(top)]
    expert_iota = lax.broadcasted_iota(jnp.int32, (1, E), 1)
    chosen_masks = [(choice == expert_iota).astype(WIDE) for choice in choices]
    flat = jnp.concatenate(choices, axis=0)
    hits = (flat == expert_iota).astype(LOW)
    pairs = (own_rows * top, own_rows * top)
    earlier = lax.broadcasted_iota(jnp.int32, pairs, 0) > lax.broadcasted_iota(jnp.int32, pairs, 1)
    before = dot(earlier.astype(LOW), hits, ((1,), (0,)))
    rank = jnp.sum(before * hits.astype(WIDE), axis=-1, keepdims=True).astype(jnp.int32)
    target = flat * capacity + rank
    slots = E * capacity
    slot_iota = lax.broadcasted_iota(jnp.int32, (1, Y * slots), 1) % slots
    route_map = (target == slot_iota).astype(LOW)
    maps = [route_map[t * own_rows : (t + 1) * own_rows] for t in range(top)]
    per_token = sum(maps[1:], maps[0])

    def exchange(rows):
        blocks = rows.reshape(Y * E, capacity, rows.shape[1])
        return every_block(blocks, LAYER).reshape(rows.shape)

    rows = dot(per_token, normed_two, ((0,), (0,)))
    router_logits = dot(normed_two, router, ((1,), (0,)))
    chosen = [jnp.sum(mask * router_logits, axis=-1, keepdims=True) for mask in chosen_masks]
    highest = chosen[0]
    for value in chosen[1:]:
        highest = jnp.maximum(highest, value)
    raised = [jnp.exp(value - highest) for value in chosen]
    gates = [value / sum(raised[1:], raised[0]) for value in raised]
    cot = cotangent[0]
    grad_picked = jnp.concatenate([(gate * cot).astype(LOW) for gate in gates], axis=0)
    grad_rows = dot(route_map, grad_picked, ((0,), (0,)))
    both = exchange(jnp.concatenate([rows, grad_rows], axis=1).astype(LOW))

    block = part_ff if part_ff % 128 == 0 else FF // Y
    results, grad_first, grad_second = expert(both, w_first, w_second, block)
    back = exchange(results)
    returned, coming = back[:, :D], back[:, D:]
    first_low = lax.psum_scatter(grad_first, "hz", scatter_dimension=0, tiled=True)
    shard_second = lax.psum_scatter(grad_second, "hz", scatter_dimension=0, tiled=True)

    picked = [dot(one, returned, ((1,), (0,))) for one in maps]
    output = resid
    for gate, rows_of in zip(gates, picked):
        output = output + gate * rows_of
    grad_gates = [jnp.sum(rows_of * cot, axis=-1, keepdims=True) for rows_of in picked]
    inner = sum(gate * grad for gate, grad in zip(gates, grad_gates))
    logit_gradient = sum(
        gate * (grad - inner) * mask
        for gate, grad, mask in zip(gates, grad_gates, chosen_masks)
    )
    grad_normed_two = dot(per_token, coming, ((1,), (0,))) + jnp.einsum(
        "te,de->td", logit_gradient, router.astype(WIDE), precision=PRECISION_FULL
    )
    grad_router = jnp.einsum(
        "td,te->de", normed_two.astype(WIDE), logit_gradient, precision=PRECISION_FULL
    )
    grad_gain_two = jnp.sum(grad_normed_two * hat_two, axis=0)
    grad_hat = grad_normed_two * gain_second
    grad_resid = cot + scale_two * (
        grad_hat - hat_two * jnp.mean(grad_hat * hat_two, axis=-1, keepdims=True)
    )
    grad_attention = grad_resid.astype(LOW)
    grad_attn_out = dot(mixed_full, grad_attention, ((0,), (0,)))
    grad_mixed = lax.dot_general(
        w_attn_out.reshape(Z, gw, D),
        grad_attention,
        (((2,), (1,)), ((), ())),
        preferred_element_type=WIDE,
    ).transpose(0, 2, 1).astype(LOW)
    grad_mixed_rows = jnp.concatenate(
        [pick(grad_mixed, z)]
        + [shift(pick(grad_mixed, (z - d) % Z), "hz", d) for d in range(1, Z)],
        axis=0,
    )

    grad_heads = by_head(grad_mixed_rows)
    row_dot = jnp.sum(
        by_head(mixed.reshape(Z * own_rows, gw)).astype(WIDE) * grad_heads.astype(WIDE),
        axis=-1,
        keepdims=True,
    )
    grad_probs = jnp.einsum("hqe,hke->hqk", grad_heads, v_heads, preferred_element_type=WIDE)
    grad_scores = (probs_low.astype(WIDE) * (grad_probs - row_dot)).astype(LOW)
    grad_q_wide = jnp.einsum(
        "hqk,hke->hqe",
        grad_scores,
        jnp.concatenate([k_heads, k_hot], axis=-1),
        preferred_element_type=WIDE,
    )
    grad_q = grad_q_wide[..., :hd] * hd**-0.5
    tile_sums = grad_q_wide[..., hd:].reshape(hg, n_q, half, n_k).sum(axis=2)
    table_part = jnp.sum(
        jnp.where(bucket_hot[None], tile_sums[..., None], 0.0), axis=(1, 2)
    )
    grad_k = jnp.einsum("hqk,hqe->khe", grad_scores, q_heads, preferred_element_type=WIDE)
    grad_v = jnp.einsum("hqk,hqe->khe", probs_low, grad_heads, preferred_element_type=WIDE)
    grad_kv = jnp.concatenate(
        [grad_k.reshape(-1, gw), grad_v.reshape(-1, gw)], axis=1
    ).reshape(Y, Z * own_rows, 2 * gw)
    grad_kv_own = grad_kv[0]
    for k in range(1, Y):
        grad_kv_own = grad_kv_own + swap(grad_kv[k].astype(LOW), ("yy",), k).astype(WIDE)
    grad_q_rows = grad_q.transpose(1, 0, 2).reshape(-1, gw)
    grad_qkv = jnp.concatenate([grad_kv_own, grad_q_rows], axis=1).astype(LOW)

    grad_normed_part = dot(grad_qkv, w_all[:, : 3 * gw], ((1,), (1,)))
    grad_low = grad_normed_part.astype(LOW).reshape(Z, own_rows, D)
    grad_normed_one = grad_normed_part[:own_rows]
    for d in range(1, Z):
        grad_normed_one = grad_normed_one + shift(grad_low[d], "hz", -d).astype(WIDE)
    def pad_columns(columns):
        return jnp.pad(columns, ((0, 0), (0, 128 - columns.shape[1])))

    attn_part = jnp.concatenate(
        [grad_attn_out, pad_columns(jnp.concatenate([grad_gain_two[:, None], grad_router], 1))],
        axis=1,
    )
    me_c = lax.axis_index("cc")
    cores = lax.axis_size("cc")
    yx = Y * E // cores

    def to_chip(part):
        split = part.astype(LOW).reshape(Z, yx, cores, shard, part.shape[1])
        split = split.transpose(2, 1, 0, 3, 4).reshape(cores, yx, Z * shard, part.shape[1])
        other = swap(pick(split, 1 - me_c), ("cc",), 1)
        return (pick(split, me_c).astype(WIDE) + other.astype(WIDE)).astype(LOW)

    attn_chip = to_chip(attn_part)

    line_rows = Z * shard
    table_size = 3 * hg * buckets

    def table_columns(table, rows):
        width = -(-table_size // rows)
        terms = jnp.pad(low_terms(table).reshape(-1), (0, rows * width - table_size))
        return terms.reshape(rows, width)

    def table_of(columns):
        terms = columns.reshape(columns.shape[0], -1)[:, :table_size]
        return terms.reshape(-1, 3, hg, buckets).sum(axis=1)

    grad_w_qkv = dot(normed_one, grad_qkv, ((0,), (0,))).astype(LOW)
    table_chip = table_part + swap(table_part, ("cc",), 1)
    table_block = table_columns(table_chip, line_rows)
    table_width = table_block.shape[1]
    extra_width = -(-(3 * gw + table_width) // 128) * 128 - 3 * gw
    table_block = jnp.pad(table_block, ((0, 0), (0, extra_width - table_width)))
    extra = jnp.broadcast_to(table_block[None], (yx, line_rows, extra_width))
    attn_width = attn_part.shape[1]
    chip_blocks = jnp.concatenate([attn_chip, to_chip(grad_w_qkv), extra], axis=2)
    got = every_block(chip_blocks, ("yy", "xx")).astype(WIDE)
    layer_sum = got[:, :, : attn_width + 3 * gw].sum(axis=0)
    attn_sum, qkv_sum = layer_sum[:, :attn_width], layer_sum[:, attn_width:]
    table_at = attn_width + 3 * gw
    layer_table = table_of(got[:, :, table_at : table_at + table_width]).sum(axis=0)
    first_low = first_low.reshape(Y, D // N, FF // Y)
    first_sent = [pick(first_low, y ^ k) for k in range(1, Y)]
    first_got = [swap(sent, ("yy",), k) for k, sent in enumerate(first_sent, 1)]
    first_parts = from_xor([pick(first_low, y)] + first_got, y)
    table_block = after(table_columns(layer_table, shard), grad_low, *first_sent)
    line_width = table_block.shape[1]
    grad_normed_one = after(grad_normed_one, *first_got)
    own_hat = hat_one[:own_rows]
    grad_hat_one = grad_normed_one * gain_first
    grad_inputs = grad_resid + scale_one[:own_rows] * (
        grad_hat_one - own_hat * jnp.mean(grad_hat_one * own_hat, axis=-1, keepdims=True)
    )
    line_blocks = jnp.concatenate(
        [
            attn_sum.astype(LOW).reshape(Z, shard, attn_width),
            qkv_sum.astype(LOW).reshape(Z, shard, 3 * gw),
            jnp.broadcast_to(table_block[None], (Z, shard, line_width)),
        ],
        axis=2,
    )
    line_pad = -(-line_blocks.shape[2] // 128) * 128 - line_blocks.shape[2]
    line_blocks = jnp.pad(line_blocks, ((0, 0), (0, 0), (0, line_pad)))
    line = every_block(line_blocks, ("hz",)).astype(WIDE)
    attn_total = line[:, :, :attn_width].sum(axis=0)
    shard_attn_out = attn_total[:, :D]
    shard_gain_two = attn_total[:, D]
    shard_router = attn_total[:, D + 1 : D + 1 + E]
    line = line[:, :, attn_width:]
    shard_qkv = jnp.concatenate(
        [line[g, :, part * gw : (part + 1) * gw] for part in (2, 0, 1) for g in range(Z)], axis=1
    )
    shard_gain_one = jnp.sum(
        shard_qkv * query_key_value_weight.astype(WIDE), axis=1
    ) / gain_one.astype(WIDE)
    tables = table_of(line[:, :, 3 * gw : 3 * gw + line_width])
    table_total = tables.reshape(heads, buckets).T

    shard_second = after(shard_second, table_block).astype(WIDE)
    shard_first = jnp.concatenate(
        [
            first_parts[k][:, g * part_ff : (g + 1) * part_ff]
            for g in range(Z)
            for k in range(Y)
        ],
        axis=1,
    ).astype(WIDE)
    return (
        output[None],
        grad_inputs[None],
        shard_gain_one,
        shard_qkv,
        shard_attn_out,
        table_total,
        shard_gain_two,
        shard_router,
        shard_first[None],
        shard_second[None],
    )


def solution(mesh):
    devices_ctx, devices_exp = mesh.shape["ctx"], mesh.shape["exp"]
    outer = 4
    parts = Mesh(
        mesh.devices.reshape(outer, devices_ctx // outer, devices_exp // 2, 2),
        ("hz", "yy", "xx", "cc"),
    )
    ctx, exp = ("hz", "yy"), ("xx", "cc")
    every = ctx + exp
    tokens = P(exp, ctx, None)
    return jax.shard_map(
        body,
        mesh=parts,
        in_specs=(
            tokens,
            P(every),
            P(every, None),
            P(every, None),
            P(),
            P(every),
            P(every, None),
            tokens,
            tokens,
            tokens,
            P(),
            tokens,
        ),
        out_specs=(
            tokens,
            tokens,
            P(every),
            P(every, None),
            P(every, None),
            P(),
            P(every),
            P(every, None),
            tokens,
            tokens,
        ),
        check_vma=False,
    )
```

```python
import jax
import jax.numpy as jnp
from jax import lax
from jax.experimental import pallas as pl
from jax.experimental.pallas import tpu as pltpu
from jax.sharding import Mesh, PartitionSpec as P

PRECISION_FULL = lax.Precision.HIGHEST
MASKED = -1e30
LOW = jnp.bfloat16
WIDE = jnp.float32
EPS = 1e-06
LAYER = ("yy", "xx", "cc")


def dot(left, right, contract):
    return lax.dot_general(left, right, (contract, ((), ())), preferred_element_type=WIDE)


def shift(x, axis, d):
    n = lax.axis_size(axis)
    return lax.ppermute(x, axis, [((j + d) % n, j) for j in range(n)])


def swap(x, axes, k):
    n = 1
    for axis in axes:
        n *= lax.axis_size(axis)
    return lax.ppermute(x, axes, [(j ^ k, j) for j in range(n)])


def from_xor(blocks, me):
    step = 1
    while step < len(blocks):
        flip = (me & step) != 0
        blocks = [jnp.where(flip, blocks[j ^ step], blocks[j]) for j in range(len(blocks))]
        step *= 2
    return blocks


def from_cyclic(blocks, me):
    n, step = len(blocks), 1
    while step < n:
        move = (me & step) != 0
        blocks = [jnp.where(move, blocks[(j - step) % n], blocks[j]) for j in range(n)]
        step *= 2
    return blocks


def after(x, *others):
    for other in others:
        first = lax.slice(other, (0,) * other.ndim, (1,) * other.ndim).reshape(())
        x = x + (first * 0).astype(x.dtype)
    return x


def expert_kernel(both, w_first, w_second, out, grad_first, grad_second, total, rows_t):
    step, steps = pl.program_id(0), pl.num_programs(0)
    width = w_first.shape[0]
    rows, grads = both[:, :width], both[:, width:]

    @pl.when(step == 0)
    def _():
        rows_t[...] = rows.T
        total[...] = jnp.zeros_like(total)

    hidden = dot(rows, w_first[...], ((1,), (0,)))
    square = hidden * hidden
    curve = jnp.tanh(0.7978845608028654 * (hidden + 0.044715 * square * hidden))
    active = (0.5 * hidden * (1.0 + curve)).astype(LOW)
    slope = 0.5 * (1.0 + curve) + 0.5 * hidden * (1.0 - curve * curve) * (
        0.7978845608028654 * (1.0 + 0.134145 * square)
    )
    total[:, :width] += dot(active, w_second[...], ((1,), (0,)))
    grad_second[...] = dot(active, grads, ((0,), (0,))).astype(LOW)
    grad_active = dot(grads, w_second[...], ((1,), (1,)))
    grad_hidden = (slope * grad_active).astype(LOW)
    total[:, width:] += dot(grad_hidden, w_first[...], ((1,), (1,)))
    grad_first[...] = dot(rows_t[...], grad_hidden, ((1,), (0,))).astype(LOW)

    @pl.when(step == steps - 1)
    def _():
        out[...] = total[...].astype(LOW)


def expert(both, w_first, w_second, block):
    count, width, units = both.shape[0], w_first.shape[0], w_first.shape[1]
    whole = pl.BlockSpec(memory_space=pltpu.VMEM)
    flops = 12 * count * width * units
    return pl.pallas_call(
        expert_kernel,
        grid=(units // block,),
        out_shape=(
            jax.ShapeDtypeStruct(both.shape, LOW),
            jax.ShapeDtypeStruct(w_first.shape, LOW),
            jax.ShapeDtypeStruct(w_second.shape, LOW),
        ),
        in_specs=[
            whole,
            pl.BlockSpec((width, block), lambda i: (0, i)),
            pl.BlockSpec((block, width), lambda i: (i, 0)),
        ],
        out_specs=(
            whole,
            pl.BlockSpec((width, block), lambda i: (0, i)),
            pl.BlockSpec((block, width), lambda i: (i, 0)),
        ),
        scratch_shapes=[pltpu.VMEM(both.shape, WIDE), pltpu.VMEM((width, count), LOW)],
        compiler_params=pltpu.CompilerParams(vmem_limit_bytes=56 * 1024 * 1024),
        cost_estimate=pl.CostEstimate(
            flops=flops, bytes_accessed=4 * both.size + 8 * w_first.size, transcendentals=count * units
        ),
    )(both, w_first, w_second)


def pick(stack, index):
    return lax.dynamic_index_in_dim(stack, index, 0, keepdims=False)


def layer_gather(block):
    yx_count = lax.axis_size("yy") * lax.axis_size("xx")
    me_yx = lax.axis_index("yy") * lax.axis_size("xx") + lax.axis_index("xx")
    blocks = [block] + [swap(block, ("yy", "xx"), k) for k in range(1, yx_count)]
    joined = jnp.stack(from_xor(blocks, me_yx))
    both = from_xor([joined, swap(joined, ("cc",), 1)], lax.axis_index("cc"))
    full = jnp.stack(both)
    cores, layers, outer, rows, width = full.shape
    return full.transpose(2, 1, 0, 3, 4).reshape(outer * layers * cores * rows, width)


def every_block(x, axes):
    return lax.all_to_all(x, axes, split_axis=0, concat_axis=0, tiled=True)


def low_terms(x):
    return jnp.concatenate(three_terms(x), axis=0)


def three_terms(x):
    high = lax.reduce_precision(x, 8, 7)
    rest = x - high
    middle = lax.reduce_precision(rest, 8, 7)
    return high.astype(LOW), middle.astype(LOW), (rest - middle).astype(LOW)


def body(
    activations,
    gain_one,
    query_key_value_weight,
    attention_output_weight,
    pos_table,
    gain_two,
    w_router,
    w_in,
    w_out,
    routes,
    pair_of_device,
    cotangent,
):
    Z, Y = lax.axis_size("hz"), lax.axis_size("yy")
    E, N = lax.axis_size("xx") * lax.axis_size("cc"), Z * Y
    z, y = lax.axis_index("hz"), lax.axis_index("yy")
    _, own_rows, D = activations.shape
    half = own_rows // 2
    buckets, heads = pos_table.shape
    hd = D // heads
    hg = heads // Z
    gw = hg * hd
    top = routes.shape[2]
    shard = gain_one.shape[0]
    FF = w_in.shape[2]
    capacity = max(2, 5 * own_rows * top // (4 * E))

    acts = activations[0]
    act_blocks = [acts] + [shift(acts, "hz", d) for d in range(1, Z)]
    small = jnp.concatenate([gain_one[:, None], gain_two[:, None], w_router], axis=1)
    small_width = -(-(gw + small.shape[1]) // 128) * 128 - gw
    small = jnp.pad(small, ((0, 0), (0, small_width - small.shape[1])))

    def qkv_piece(group):
        columns = [
            lax.dynamic_slice(query_key_value_weight, (0, part * D + group * gw), (shard, gw))
            for part in (1, 2, 0)
        ]
        return jnp.concatenate(columns + [small, attention_output_weight], axis=1)

    pieces = [qkv_piece(z)] + [shift(qkv_piece((z - d) % Z), "hz", d) for d in range(1, Z)]
    pieces_in_line = jnp.stack(from_cyclic(pieces, z))
    w_all = layer_gather(pieces_in_line[:, :, : gw * 3 + small_width])

    w_second = lax.all_gather(w_out[0], "hz", axis=0, tiled=True)
    part_ff = FF // N

    def in_piece(part):
        columns = [
            lax.dynamic_slice(w_in[0], (0, (g * Y + part) * part_ff), (D // N, part_ff))
            for g in range(Z)
        ]
        return jnp.concatenate(columns, axis=1)

    in_rows = [in_piece(y)] + [
        swap(after(in_piece(y ^ k), pieces[1]), ("yy",), k) for k in range(1, Y)
    ]
    in_rows = lax.optimization_barrier(jnp.concatenate(from_xor(in_rows, y), axis=0))
    w_first = lax.all_gather(in_rows, "hz", axis=0, tiled=True)

    gain_first = w_all[:, 3 * gw].astype(WIDE)
    gain_second = w_all[:, 3 * gw + 1].astype(WIDE)
    router = w_all[:, 3 * gw + 2 : 3 * gw + 2 + E]

    n_q, n_k = 2 * Z, 2 * Z * Y

    def tile_of(count, width, axis):
        shape = (count, 1) if axis == 0 else (1, count)
        entry = lax.broadcasted_iota(jnp.int32, shape, axis) // width
        owner = ((z + (entry // 2) % Z) % Z) * Y + (y ^ (entry // (2 * Z)))
        hot_shape = (count, N) if axis == 0 else (N, count)
        lanes = lax.broadcasted_iota(jnp.int32, hot_shape, 1 - axis)
        pairs = pair_of_device[None, :] if axis == 0 else pair_of_device[:, None]
        first = jnp.sum(jnp.where(lanes == owner, pairs, 0), axis=1 - axis, keepdims=True)
        return jnp.where(entry % 2 == 0, first, 2 * N - 1 - first)

    def position_of(count, axis):
        shape = (count, 1) if axis == 0 else (1, count)
        within = lax.broadcasted_iota(jnp.int32, shape, axis) % half
        return tile_of(count, half, axis) * half + within

    query_pos = position_of(n_q * half, 0)
    key_pos = position_of(n_k * half, 1)
    bucket = jnp.clip(tile_of(n_q, 1, 0) - tile_of(n_k, 1, 1), 0, buckets - 1)
    levels = lax.broadcasted_iota(jnp.int32, (n_q, n_k, buckets), 2)
    bucket_hot = bucket[:, :, None] == levels
    own_table = lax.dynamic_slice(pos_table, (0, z * hg), (buckets, hg)).T
    tile_bias = jnp.sum(jnp.where(bucket_hot[None], own_table[:, None, None, :], 0.0), axis=-1)
    bias_terms = jnp.concatenate(three_terms(tile_bias), axis=-1)
    bias_rows = jnp.broadcast_to(
        bias_terms[:, :, None, :], (hg, n_q, half, 3 * n_k)
    ).reshape(hg, n_q * half, 3 * n_k)
    key_hot = (
        lax.broadcasted_iota(jnp.int32, (n_k * half, n_k), 0) // half
        == lax.broadcasted_iota(jnp.int32, (n_k * half, n_k), 1)
    ).astype(LOW)

    x_rows = jnp.concatenate(act_blocks, axis=0).astype(WIDE)
    scale_one = lax.rsqrt(jnp.mean(x_rows * x_rows, axis=-1, keepdims=True) + EPS)
    hat_one = x_rows * scale_one
    normed_one = (hat_one * gain_first).astype(LOW)
    w_kv, w_q = w_all[:, : 2 * gw], w_all[:, 2 * gw : 3 * gw]
    kv = dot(normed_one, w_kv, ((1,), (0,))).astype(LOW)
    attn_pieces = after(pieces_in_line[:, :, 3 * gw + small_width :], kv)
    w_attn_out = layer_gather(attn_pieces)
    kv_all = jnp.concatenate([kv] + [swap(kv, ("yy",), k) for k in range(1, Y)], axis=0)
    q = dot(normed_one, w_q, ((1,), (0,))).astype(LOW)

    def by_head(rows):
        return rows.reshape(rows.shape[0], hg, hd).transpose(1, 0, 2)

    bias_rows = after(bias_rows, in_rows)
    q_heads = by_head(q) * jnp.asarray(hd**-0.5, LOW)
    k_heads, v_heads = by_head(kv_all[:, :gw]), by_head(kv_all[:, gw:])
    q_wide = jnp.concatenate([q_heads, bias_rows], axis=-1)
    k_hot = jnp.broadcast_to(key_hot[None], (hg,) + key_hot.shape)
    k_wide = jnp.concatenate([k_heads, k_hot, k_hot, k_hot], axis=-1)
    scores = jnp.einsum("hqe,hke->hqk", q_wide, k_wide, preferred_element_type=WIDE)
    visible = query_pos >= key_pos
    scores = jnp.where(visible[None], scores, MASKED)
    weights = jnp.exp(scores - jnp.max(scores, axis=-1, keepdims=True))
    probs = weights / jnp.sum(weights, axis=-1, keepdims=True)
    probs_low = probs.astype(LOW)
    mixed_heads = jnp.einsum("hqk,hke->qhe", probs_low, v_heads, preferred_element_type=WIDE)
    mixed = mixed_heads.reshape(Z, own_rows, gw).astype(LOW)
    mixed_back = [mixed[0]] + [shift(mixed[d], "hz", -d) for d in range(1, Z)]
    mixed_back = from_cyclic([mixed_back[-d % Z] for d in range(Z)], z)
    mixed_full = jnp.concatenate(mixed_back, axis=-1)

    own_x = acts.astype(WIDE)
    resid = own_x + dot(mixed_full, w_attn_out, ((1,), (0,)))
    scale_two = lax.rsqrt(jnp.mean(resid * resid, axis=-1, keepdims=True) + EPS)
    hat_two = resid * scale_two
    normed_two = (hat_two * gain_second).astype(LOW)

    choices = [routes[0][:, t : t + 1] for t in range(top)]
    expert_iota = lax.broadcasted_iota(jnp.int32, (1, E), 1)
    chosen_masks = [(choice == expert_iota).astype(WIDE) for choice in choices]
    flat = jnp.concatenate(choices, axis=0)
    hits = (flat == expert_iota).astype(LOW)
    pairs = (own_rows * top, own_rows * top)
    earlier = lax.broadcasted_iota(jnp.int32, pairs, 0) > lax.broadcasted_iota(jnp.int32, pairs, 1)
    before = dot(earlier.astype(LOW), hits, ((1,), (0,)))
    rank = jnp.sum(before * hits.astype(WIDE), axis=-1, keepdims=True).astype(jnp.int32)
    target = flat * capacity + rank
    slots = E * capacity
    slot_iota = lax.broadcasted_iota(jnp.int32, (1, Y * slots), 1) % slots
    route_map = (target == slot_iota).astype(LOW)
    maps = [route_map[t * own_rows : (t + 1) * own_rows] for t in range(top)]
    per_token = sum(maps[1:], maps[0])

    def exchange(rows):
        blocks = rows.reshape(Y * E, capacity, rows.shape[1])
        return every_block(blocks, LAYER).reshape(rows.shape)

    rows = dot(per_token, normed_two, ((0,), (0,)))
    router_logits = dot(normed_two, router, ((1,), (0,)))
    chosen = [jnp.sum(mask * router_logits, axis=-1, keepdims=True) for mask in chosen_masks]
    highest = chosen[0]
    for value in chosen[1:]:
        highest = jnp.maximum(highest, value)
    raised = [jnp.exp(value - highest) for value in chosen]
    gates = [value / sum(raised[1:], raised[0]) for value in raised]
    cot = cotangent[0]
    grad_picked = jnp.concatenate([(gate * cot).astype(LOW) for gate in gates], axis=0)
    grad_rows = dot(route_map, grad_picked, ((0,), (0,)))
    both = exchange(jnp.concatenate([rows, grad_rows], axis=1).astype(LOW))

    block = 512 if (FF // Y) % 512 == 0 else FF // Y
    results, grad_first, grad_second = expert(both, w_first, w_second, block)
    back = exchange(results)
    returned, coming = back[:, :D], back[:, D:]
    first_low = lax.psum_scatter(grad_first, "hz", scatter_dimension=0, tiled=True)
    shard_second = lax.psum_scatter(grad_second, "hz", scatter_dimension=0, tiled=True)

    picked = [dot(one, returned, ((1,), (0,))) for one in maps]
    output = resid
    for gate, rows_of in zip(gates, picked):
        output = output + gate * rows_of
    grad_gates = [jnp.sum(rows_of * cot, axis=-1, keepdims=True) for rows_of in picked]
    inner = sum(gate * grad for gate, grad in zip(gates, grad_gates))
    logit_gradient = sum(
        gate * (grad - inner) * mask
        for gate, grad, mask in zip(gates, grad_gates, chosen_masks)
    )
    grad_normed_two = dot(per_token, coming, ((1,), (0,))) + jnp.einsum(
        "te,de->td", logit_gradient, router.astype(WIDE), precision=PRECISION_FULL
    )
    grad_router = jnp.einsum(
        "td,te->de", normed_two.astype(WIDE), logit_gradient, precision=PRECISION_FULL
    )
    grad_gain_two = jnp.sum(grad_normed_two * hat_two, axis=0)
    grad_hat = grad_normed_two * gain_second
    grad_resid = cot + scale_two * (
        grad_hat - hat_two * jnp.mean(grad_hat * hat_two, axis=-1, keepdims=True)
    )
    grad_attention = grad_resid.astype(LOW)
    grad_attn_out = dot(mixed_full, grad_attention, ((0,), (0,)))
    grad_mixed = lax.dot_general(
        w_attn_out.reshape(Z, gw, D),
        grad_attention,
        (((2,), (1,)), ((), ())),
        preferred_element_type=WIDE,
    ).transpose(0, 2, 1).astype(LOW)
    grad_mixed_rows = jnp.concatenate(
        [pick(grad_mixed, z)]
        + [shift(pick(grad_mixed, (z - d) % Z), "hz", d) for d in range(1, Z)],
        axis=0,
    )

    grad_heads = by_head(grad_mixed_rows)
    row_dot = jnp.sum(
        by_head(mixed.reshape(Z * own_rows, gw)).astype(WIDE) * grad_heads.astype(WIDE),
        axis=-1,
        keepdims=True,
    )
    grad_probs = jnp.einsum("hqe,hke->hqk", grad_heads, v_heads, preferred_element_type=WIDE)
    grad_scores = (probs_low.astype(WIDE) * (grad_probs - row_dot)).astype(LOW)
    grad_q_wide = jnp.einsum(
        "hqk,hke->hqe",
        grad_scores,
        jnp.concatenate([k_heads, k_hot], axis=-1),
        preferred_element_type=WIDE,
    )
    grad_q = grad_q_wide[..., :hd] * hd**-0.5
    tile_sums = grad_q_wide[..., hd:].reshape(hg, n_q, half, n_k).sum(axis=2)
    table_part = jnp.sum(
        jnp.where(bucket_hot[None], tile_sums[..., None], 0.0), axis=(1, 2)
    )
    grad_k = jnp.einsum("hqk,hqe->khe", grad_scores, q_heads, preferred_element_type=WIDE)
    grad_v = jnp.einsum("hqk,hqe->khe", probs_low, grad_heads, preferred_element_type=WIDE)
    grad_kv = jnp.concatenate(
        [grad_k.reshape(-1, gw), grad_v.reshape(-1, gw)], axis=1
    ).reshape(Y, Z * own_rows, 2 * gw)
    grad_kv_own = grad_kv[0]
    for k in range(1, Y):
        grad_kv_own = grad_kv_own + swap(grad_kv[k].astype(LOW), ("yy",), k).astype(WIDE)
    grad_q_rows = grad_q.transpose(1, 0, 2).reshape(-1, gw)
    grad_qkv = jnp.concatenate([grad_kv_own, grad_q_rows], axis=1).astype(LOW)

    grad_normed_part = dot(grad_qkv, w_all[:, : 3 * gw], ((1,), (1,)))
    grad_low = grad_normed_part.astype(LOW).reshape(Z, own_rows, D)
    grad_normed_one = grad_normed_part[:own_rows]
    for d in range(1, Z):
        grad_normed_one = grad_normed_one + shift(grad_low[d], "hz", -d).astype(WIDE)
    def pad_columns(columns):
        return jnp.pad(columns, ((0, 0), (0, 128 - columns.shape[1])))

    attn_part = jnp.concatenate(
        [grad_attn_out, pad_columns(jnp.concatenate([grad_gain_two[:, None], grad_router], 1))],
        axis=1,
    )
    me_c = lax.axis_index("cc")
    cores = lax.axis_size("cc")
    yx = Y * E // cores

    def to_chip(part):
        split = part.astype(LOW).reshape(Z, yx, cores, shard, part.shape[1])
        split = split.transpose(2, 1, 0, 3, 4).reshape(cores, yx, Z * shard, part.shape[1])
        other = swap(pick(split, 1 - me_c), ("cc",), 1)
        return (pick(split, me_c).astype(WIDE) + other.astype(WIDE)).astype(LOW)

    attn_chip = to_chip(attn_part)

    line_rows = Z * shard
    table_size = 3 * hg * buckets

    def table_columns(table, rows):
        width = -(-table_size // rows)
        terms = jnp.pad(low_terms(table).reshape(-1), (0, rows * width - table_size))
        return terms.reshape(rows, width)

    def table_of(columns):
        terms = columns.reshape(columns.shape[0], -1)[:, :table_size]
        return terms.reshape(-1, 3, hg, buckets).sum(axis=1)

    grad_w_qkv = dot(normed_one, grad_qkv, ((0,), (0,))).astype(LOW)
    table_chip = table_part + swap(table_part, ("cc",), 1)
    table_block = table_columns(table_chip, line_rows)
    table_width = table_block.shape[1]
    extra_width = -(-(3 * gw + table_width) // 128) * 128 - 3 * gw
    table_block = jnp.pad(table_block, ((0, 0), (0, extra_width - table_width)))
    extra = jnp.broadcast_to(table_block[None], (yx, line_rows, extra_width))
    attn_width = attn_part.shape[1]
    chip_blocks = jnp.concatenate([attn_chip, to_chip(grad_w_qkv), extra], axis=2)
    got = every_block(chip_blocks, ("yy", "xx")).astype(WIDE)
    layer_sum = got[:, :, : attn_width + 3 * gw].sum(axis=0)
    attn_sum, qkv_sum = layer_sum[:, :attn_width], layer_sum[:, attn_width:]
    table_at = attn_width + 3 * gw
    layer_table = table_of(got[:, :, table_at : table_at + table_width]).sum(axis=0)
    first_low = first_low.reshape(Y, D // N, FF // Y)
    first_sent = [pick(first_low, y ^ k) for k in range(1, Y)]
    first_got = [swap(sent, ("yy",), k) for k, sent in enumerate(first_sent, 1)]
    first_parts = from_xor([pick(first_low, y)] + first_got, y)
    table_block = after(table_columns(layer_table, shard), grad_low, *first_sent)
    line_width = table_block.shape[1]
    grad_normed_one = after(grad_normed_one, *first_got)
    own_hat = hat_one[:own_rows]
    grad_hat_one = grad_normed_one * gain_first
    grad_inputs = grad_resid + scale_one[:own_rows] * (
        grad_hat_one - own_hat * jnp.mean(grad_hat_one * own_hat, axis=-1, keepdims=True)
    )
    line_blocks = jnp.concatenate(
        [
            attn_sum.astype(LOW).reshape(Z, shard, attn_width),
            qkv_sum.astype(LOW).reshape(Z, shard, 3 * gw),
            jnp.broadcast_to(table_block[None], (Z, shard, line_width)),
        ],
        axis=2,
    )
    line_pad = -(-line_blocks.shape[2] // 128) * 128 - line_blocks.shape[2]
    line_blocks = jnp.pad(line_blocks, ((0, 0), (0, 0), (0, line_pad)))
    line = every_block(line_blocks, ("hz",)).astype(WIDE)
    attn_total = line[:, :, :attn_width].sum(axis=0)
    shard_attn_out = attn_total[:, :D]
    shard_gain_two = attn_total[:, D]
    shard_router = attn_total[:, D + 1 : D + 1 + E]
    line = line[:, :, attn_width:]
    shard_qkv = jnp.concatenate(
        [line[g, :, part * gw : (part + 1) * gw] for part in (2, 0, 1) for g in range(Z)], axis=1
    )
    shard_gain_one = jnp.sum(
        shard_qkv * query_key_value_weight.astype(WIDE), axis=1
    ) / gain_one.astype(WIDE)
    tables = table_of(line[:, :, 3 * gw : 3 * gw + line_width])
    table_total = tables.reshape(heads, buckets).T

    shard_second = after(shard_second, table_block).astype(WIDE)
    shard_first = jnp.concatenate(
        [
            first_parts[k][:, g * part_ff : (g + 1) * part_ff]
            for g in range(Z)
            for k in range(Y)
        ],
        axis=1,
    ).astype(WIDE)
    return (
        output[None],
        grad_inputs[None],
        shard_gain_one,
        shard_qkv,
        shard_attn_out,
        table_total,
        shard_gain_two,
        shard_router,
        shard_first[None],
        shard_second[None],
    )


def solution(mesh):
    devices_ctx, devices_exp = mesh.shape["ctx"], mesh.shape["exp"]
    outer = 4
    parts = Mesh(
        mesh.devices.reshape(outer, devices_ctx // outer, devices_exp // 2, 2),
        ("hz", "yy", "xx", "cc"),
    )
    ctx, exp = ("hz", "yy"), ("xx", "cc")
    every = ctx + exp
    tokens = P(exp, ctx, None)
    return jax.shard_map(
        body,
        mesh=parts,
        in_specs=(
            tokens,
            P(every),
            P(every, None),
            P(every, None),
            P(),
            P(every),
            P(every, None),
            tokens,
            tokens,
            tokens,
            P(),
            tokens,
        ),
        out_specs=(
            tokens,
            tokens,
            P(every),
            P(every, None),
            P(every, None),
            P(),
            P(every),
            P(every, None),
            tokens,
            tokens,
        ),
        check_vma=False,
    )
```

```python
import jax
import jax.numpy as jnp
from jax import lax
from jax.experimental import pallas as pl
from jax.experimental.pallas import tpu as pltpu
from jax.sharding import Mesh, PartitionSpec as P

PRECISION_FULL = lax.Precision.HIGHEST
MASKED = -1e30
LOW = jnp.bfloat16
WIDE = jnp.float32
EPS = 1e-06
LAYER = ("yy", "xx", "cc")


def dot(left, right, contract):
    return lax.dot_general(left, right, (contract, ((), ())), preferred_element_type=WIDE)


def shift(x, axis, d):
    n = lax.axis_size(axis)
    return lax.ppermute(x, axis, [((j + d) % n, j) for j in range(n)])


def swap(x, axes, k):
    n = 1
    for axis in axes:
        n *= lax.axis_size(axis)
    return lax.ppermute(x, axes, [(j ^ k, j) for j in range(n)])


def from_xor(blocks, me):
    step = 1
    while step < len(blocks):
        flip = (me & step) != 0
        blocks = [jnp.where(flip, blocks[j ^ step], blocks[j]) for j in range(len(blocks))]
        step *= 2
    return blocks


def from_cyclic(blocks, me):
    n, step = len(blocks), 1
    while step < n:
        move = (me & step) != 0
        blocks = [jnp.where(move, blocks[(j - step) % n], blocks[j]) for j in range(n)]
        step *= 2
    return blocks


def after(x, *others):
    for other in others:
        first = lax.slice(other, (0,) * other.ndim, (1,) * other.ndim).reshape(())
        x = x + (first * 0).astype(x.dtype)
    return x


def expert_kernel(both, w_first, w_second, out, grad_first, grad_second, total, rows_t):
    step, steps = pl.program_id(0), pl.num_programs(0)
    width = w_first.shape[0]
    rows, grads = both[:, :width], both[:, width:]

    @pl.when(step == 0)
    def _():
        rows_t[...] = rows.T
        total[...] = jnp.zeros_like(total)

    hidden = dot(rows, w_first[...], ((1,), (0,)))
    square = hidden * hidden
    curve = jnp.tanh(0.7978845608028654 * (hidden + 0.044715 * square * hidden))
    active = (0.5 * hidden * (1.0 + curve)).astype(LOW)
    slope = 0.5 * (1.0 + curve) + 0.5 * hidden * (1.0 - curve * curve) * (
        0.7978845608028654 * (1.0 + 0.134145 * square)
    )
    total[:, :width] += dot(active, w_second[...], ((1,), (0,)))
    grad_second[...] = dot(active, grads, ((0,), (0,))).astype(LOW)
    grad_active = dot(grads, w_second[...], ((1,), (1,)))
    grad_hidden = (slope * grad_active).astype(LOW)
    total[:, width:] += dot(grad_hidden, w_first[...], ((1,), (1,)))
    grad_first[...] = dot(rows_t[...], grad_hidden, ((1,), (0,))).astype(LOW)

    @pl.when(step == steps - 1)
    def _():
        out[...] = total[...].astype(LOW)


def expert(both, w_first, w_second, block):
    count, width, units = both.shape[0], w_first.shape[0], w_first.shape[1]
    whole = pl.BlockSpec(memory_space=pltpu.VMEM)
    flops = 12 * count * width * units
    return pl.pallas_call(
        expert_kernel,
        grid=(units // block,),
        out_shape=(
            jax.ShapeDtypeStruct(both.shape, LOW),
            jax.ShapeDtypeStruct(w_first.shape, LOW),
            jax.ShapeDtypeStruct(w_second.shape, LOW),
        ),
        in_specs=[
            whole,
            pl.BlockSpec((width, block), lambda i: (0, i)),
            pl.BlockSpec((block, width), lambda i: (i, 0)),
        ],
        out_specs=(
            whole,
            pl.BlockSpec((width, block), lambda i: (0, i)),
            pl.BlockSpec((block, width), lambda i: (i, 0)),
        ),
        scratch_shapes=[pltpu.VMEM(both.shape, WIDE), pltpu.VMEM((width, count), LOW)],
        compiler_params=pltpu.CompilerParams(vmem_limit_bytes=(44 if count <= 1024 else 56) * 1024 * 1024),
        cost_estimate=pl.CostEstimate(
            flops=flops, bytes_accessed=4 * both.size + 8 * w_first.size, transcendentals=count * units
        ),
    )(both, w_first, w_second)


def pick(stack, index):
    return lax.dynamic_index_in_dim(stack, index, 0, keepdims=False)


def layer_gather(block):
    yx_count = lax.axis_size("yy") * lax.axis_size("xx")
    me_yx = lax.axis_index("yy") * lax.axis_size("xx") + lax.axis_index("xx")
    blocks = [block] + [swap(block, ("yy", "xx"), k) for k in range(1, yx_count)]
    joined = jnp.stack(from_xor(blocks, me_yx))
    both = from_xor([joined, swap(joined, ("cc",), 1)], lax.axis_index("cc"))
    full = jnp.stack(both)
    cores, layers, outer, rows, width = full.shape
    return full.transpose(2, 1, 0, 3, 4).reshape(outer * layers * cores * rows, width)


def every_block(x, axes):
    return lax.all_to_all(x, axes, split_axis=0, concat_axis=0, tiled=True)


def low_terms(x):
    return jnp.concatenate(three_terms(x), axis=0)


def three_terms(x):
    high = lax.reduce_precision(x, 8, 7)
    rest = x - high
    middle = lax.reduce_precision(rest, 8, 7)
    return high.astype(LOW), middle.astype(LOW), (rest - middle).astype(LOW)


def body(
    activations,
    gain_one,
    query_key_value_weight,
    attention_output_weight,
    pos_table,
    gain_two,
    w_router,
    w_in,
    w_out,
    routes,
    pair_of_device,
    cotangent,
):
    Z, Y = lax.axis_size("hz"), lax.axis_size("yy")
    E, N = lax.axis_size("xx") * lax.axis_size("cc"), Z * Y
    z, y = lax.axis_index("hz"), lax.axis_index("yy")
    _, own_rows, D = activations.shape
    half = own_rows // 2
    buckets, heads = pos_table.shape
    hd = D // heads
    hg = heads // Z
    gw = hg * hd
    top = routes.shape[2]
    shard = gain_one.shape[0]
    FF = w_in.shape[2]
    capacity = max(2, 5 * own_rows * top // (4 * E))

    acts = activations[0]
    act_blocks = [acts] + [shift(acts, "hz", d) for d in range(1, Z)]
    small = jnp.concatenate([gain_one[:, None], gain_two[:, None], w_router], axis=1)
    small_width = -(-(gw + small.shape[1]) // 128) * 128 - gw
    small = jnp.pad(small, ((0, 0), (0, small_width - small.shape[1])))

    def qkv_piece(group):
        columns = [
            lax.dynamic_slice(query_key_value_weight, (0, part * D + group * gw), (shard, gw))
            for part in (1, 2, 0)
        ]
        return jnp.concatenate(columns + [small, attention_output_weight], axis=1)

    pieces = [qkv_piece(z)] + [shift(qkv_piece((z - d) % Z), "hz", d) for d in range(1, Z)]
    pieces_in_line = jnp.stack(from_cyclic(pieces, z))
    w_all = layer_gather(pieces_in_line[:, :, : gw * 3 + small_width])

    w_second = lax.all_gather(w_out[0], "hz", axis=0, tiled=True)
    part_ff = FF // N

    def in_piece(part):
        columns = [
            lax.dynamic_slice(w_in[0], (0, (g * Y + part) * part_ff), (D // N, part_ff))
            for g in range(Z)
        ]
        return jnp.concatenate(columns, axis=1)

    in_rows = [in_piece(y)] + [
        swap(after(in_piece(y ^ k), pieces[1]), ("yy",), k) for k in range(1, Y)
    ]
    in_rows = lax.optimization_barrier(jnp.concatenate(from_xor(in_rows, y), axis=0))
    w_first = lax.all_gather(in_rows, "hz", axis=0, tiled=True)

    gain_first = w_all[:, 3 * gw].astype(WIDE)
    gain_second = w_all[:, 3 * gw + 1].astype(WIDE)
    router = w_all[:, 3 * gw + 2 : 3 * gw + 2 + E]

    n_q, n_k = 2 * Z, 2 * Z * Y

    def tile_of(count, width, axis):
        shape = (count, 1) if axis == 0 else (1, count)
        entry = lax.broadcasted_iota(jnp.int32, shape, axis) // width
        owner = ((z + (entry // 2) % Z) % Z) * Y + (y ^ (entry // (2 * Z)))
        hot_shape = (count, N) if axis == 0 else (N, count)
        lanes = lax.broadcasted_iota(jnp.int32, hot_shape, 1 - axis)
        pairs = pair_of_device[None, :] if axis == 0 else pair_of_device[:, None]
        first = jnp.sum(jnp.where(lanes == owner, pairs, 0), axis=1 - axis, keepdims=True)
        return jnp.where(entry % 2 == 0, first, 2 * N - 1 - first)

    def position_of(count, axis):
        shape = (count, 1) if axis == 0 else (1, count)
        within = lax.broadcasted_iota(jnp.int32, shape, axis) % half
        return tile_of(count, half, axis) * half + within

    query_pos = position_of(n_q * half, 0)
    key_pos = position_of(n_k * half, 1)
    bucket = jnp.clip(tile_of(n_q, 1, 0) - tile_of(n_k, 1, 1), 0, buckets - 1)
    levels = lax.broadcasted_iota(jnp.int32, (n_q, n_k, buckets), 2)
    bucket_hot = bucket[:, :, None] == levels
    own_table = lax.dynamic_slice(pos_table, (0, z * hg), (buckets, hg)).T
    tile_bias = jnp.sum(jnp.where(bucket_hot[None], own_table[:, None, None, :], 0.0), axis=-1)
    bias_terms = jnp.concatenate(three_terms(tile_bias), axis=-1)
    bias_rows = jnp.broadcast_to(
        bias_terms[:, :, None, :], (hg, n_q, half, 3 * n_k)
    ).reshape(hg, n_q * half, 3 * n_k)
    key_hot = (
        lax.broadcasted_iota(jnp.int32, (n_k * half, n_k), 0) // half
        == lax.broadcasted_iota(jnp.int32, (n_k * half, n_k), 1)
    ).astype(LOW)

    x_rows = jnp.concatenate(act_blocks, axis=0).astype(WIDE)
    scale_one = lax.rsqrt(jnp.mean(x_rows * x_rows, axis=-1, keepdims=True) + EPS)
    hat_one = x_rows * scale_one
    normed_one = (hat_one * gain_first).astype(LOW)
    w_kv, w_q = w_all[:, : 2 * gw], w_all[:, 2 * gw : 3 * gw]
    kv = dot(normed_one, w_kv, ((1,), (0,))).astype(LOW)
    attn_pieces = after(pieces_in_line[:, :, 3 * gw + small_width :], kv)
    w_attn_out = layer_gather(attn_pieces)
    kv_all = jnp.concatenate([kv] + [swap(kv, ("yy",), k) for k in range(1, Y)], axis=0)
    q = dot(normed_one, w_q, ((1,), (0,))).astype(LOW)

    def by_head(rows):
        return rows.reshape(rows.shape[0], hg, hd).transpose(1, 0, 2)

    bias_rows = after(bias_rows, in_rows)
    q_heads = by_head(q) * jnp.asarray(hd**-0.5, LOW)
    k_heads, v_heads = by_head(kv_all[:, :gw]), by_head(kv_all[:, gw:])
    q_wide = jnp.concatenate([q_heads, bias_rows], axis=-1)
    k_hot = jnp.broadcast_to(key_hot[None], (hg,) + key_hot.shape)
    k_wide = jnp.concatenate([k_heads, k_hot, k_hot, k_hot], axis=-1)
    scores = jnp.einsum("hqe,hke->hqk", q_wide, k_wide, preferred_element_type=WIDE)
    visible = query_pos >= key_pos
    scores = jnp.where(visible[None], scores, MASKED)
    weights = jnp.exp(scores - jnp.max(scores, axis=-1, keepdims=True))
    probs = weights / jnp.sum(weights, axis=-1, keepdims=True)
    probs_low = probs.astype(LOW)
    mixed_heads = jnp.einsum("hqk,hke->qhe", probs_low, v_heads, preferred_element_type=WIDE)
    mixed = mixed_heads.reshape(Z, own_rows, gw).astype(LOW)
    mixed_back = [mixed[0]] + [shift(mixed[d], "hz", -d) for d in range(1, Z)]
    mixed_back = from_cyclic([mixed_back[-d % Z] for d in range(Z)], z)
    mixed_full = jnp.concatenate(mixed_back, axis=-1)

    own_x = acts.astype(WIDE)
    resid = own_x + dot(mixed_full, w_attn_out, ((1,), (0,)))
    scale_two = lax.rsqrt(jnp.mean(resid * resid, axis=-1, keepdims=True) + EPS)
    hat_two = resid * scale_two
    normed_two = (hat_two * gain_second).astype(LOW)

    choices = [routes[0][:, t : t + 1] for t in range(top)]
    expert_iota = lax.broadcasted_iota(jnp.int32, (1, E), 1)
    chosen_masks = [(choice == expert_iota).astype(WIDE) for choice in choices]
    flat = jnp.concatenate(choices, axis=0)
    hits = (flat == expert_iota).astype(LOW)
    pairs = (own_rows * top, own_rows * top)
    earlier = lax.broadcasted_iota(jnp.int32, pairs, 0) > lax.broadcasted_iota(jnp.int32, pairs, 1)
    before = dot(earlier.astype(LOW), hits, ((1,), (0,)))
    rank = jnp.sum(before * hits.astype(WIDE), axis=-1, keepdims=True).astype(jnp.int32)
    target = flat * capacity + rank
    slots = E * capacity
    slot_iota = lax.broadcasted_iota(jnp.int32, (1, Y * slots), 1) % slots
    route_map = (target == slot_iota).astype(LOW)
    maps = [route_map[t * own_rows : (t + 1) * own_rows] for t in range(top)]
    per_token = sum(maps[1:], maps[0])

    def exchange(rows):
        blocks = rows.reshape(Y * E, capacity, rows.shape[1])
        return every_block(blocks, LAYER).reshape(rows.shape)

    rows = dot(per_token, normed_two, ((0,), (0,)))
    router_logits = dot(normed_two, router, ((1,), (0,)))
    chosen = [jnp.sum(mask * router_logits, axis=-1, keepdims=True) for mask in chosen_masks]
    highest = chosen[0]
    for value in chosen[1:]:
        highest = jnp.maximum(highest, value)
    raised = [jnp.exp(value - highest) for value in chosen]
    gates = [value / sum(raised[1:], raised[0]) for value in raised]
    cot = cotangent[0]
    grad_picked = jnp.concatenate([(gate * cot).astype(LOW) for gate in gates], axis=0)
    grad_rows = dot(route_map, grad_picked, ((0,), (0,)))
    both = exchange(jnp.concatenate([rows, grad_rows], axis=1).astype(LOW))

    block = 512 if (FF // Y) % 512 == 0 else FF // Y
    results, grad_first, grad_second = expert(both, w_first, w_second, block)
    back = exchange(results)
    returned, coming = back[:, :D], back[:, D:]
    first_low = lax.psum_scatter(grad_first, "hz", scatter_dimension=0, tiled=True)
    shard_second = lax.psum_scatter(grad_second, "hz", scatter_dimension=0, tiled=True)

    picked = [dot(one, returned, ((1,), (0,))) for one in maps]
    output = resid
    for gate, rows_of in zip(gates, picked):
        output = output + gate * rows_of
    grad_gates = [jnp.sum(rows_of * cot, axis=-1, keepdims=True) for rows_of in picked]
    inner = sum(gate * grad for gate, grad in zip(gates, grad_gates))
    logit_gradient = sum(
        gate * (grad - inner) * mask
        for gate, grad, mask in zip(gates, grad_gates, chosen_masks)
    )
    grad_normed_two = dot(per_token, coming, ((1,), (0,))) + jnp.einsum(
        "te,de->td", logit_gradient, router.astype(WIDE), precision=PRECISION_FULL
    )
    grad_router = jnp.einsum(
        "td,te->de", normed_two.astype(WIDE), logit_gradient, precision=PRECISION_FULL
    )
    grad_gain_two = jnp.sum(grad_normed_two * hat_two, axis=0)
    grad_hat = grad_normed_two * gain_second
    grad_resid = cot + scale_two * (
        grad_hat - hat_two * jnp.mean(grad_hat * hat_two, axis=-1, keepdims=True)
    )
    grad_attention = grad_resid.astype(LOW)
    grad_attn_out = dot(mixed_full, grad_attention, ((0,), (0,)))
    grad_mixed = lax.dot_general(
        w_attn_out.reshape(Z, gw, D),
        grad_attention,
        (((2,), (1,)), ((), ())),
        preferred_element_type=WIDE,
    ).transpose(0, 2, 1).astype(LOW)
    grad_mixed_rows = jnp.concatenate(
        [pick(grad_mixed, z)]
        + [shift(pick(grad_mixed, (z - d) % Z), "hz", d) for d in range(1, Z)],
        axis=0,
    )

    grad_heads = by_head(grad_mixed_rows)
    row_dot = jnp.sum(
        by_head(mixed.reshape(Z * own_rows, gw)).astype(WIDE) * grad_heads.astype(WIDE),
        axis=-1,
        keepdims=True,
    )
    grad_probs = jnp.einsum("hqe,hke->hqk", grad_heads, v_heads, preferred_element_type=WIDE)
    grad_scores = (probs_low.astype(WIDE) * (grad_probs - row_dot)).astype(LOW)
    grad_q_wide = jnp.einsum(
        "hqk,hke->hqe",
        grad_scores,
        jnp.concatenate([k_heads, k_hot], axis=-1),
        preferred_element_type=WIDE,
    )
    grad_q = grad_q_wide[..., :hd] * hd**-0.5
    tile_sums = grad_q_wide[..., hd:].reshape(hg, n_q, half, n_k).sum(axis=2)
    table_part = jnp.sum(
        jnp.where(bucket_hot[None], tile_sums[..., None], 0.0), axis=(1, 2)
    )
    grad_k = jnp.einsum("hqk,hqe->khe", grad_scores, q_heads, preferred_element_type=WIDE)
    grad_v = jnp.einsum("hqk,hqe->khe", probs_low, grad_heads, preferred_element_type=WIDE)
    grad_kv = jnp.concatenate(
        [grad_k.reshape(-1, gw), grad_v.reshape(-1, gw)], axis=1
    ).reshape(Y, Z * own_rows, 2 * gw)
    grad_kv_own = grad_kv[0]
    for k in range(1, Y):
        grad_kv_own = grad_kv_own + swap(grad_kv[k].astype(LOW), ("yy",), k).astype(WIDE)
    grad_q_rows = grad_q.transpose(1, 0, 2).reshape(-1, gw)
    grad_qkv = jnp.concatenate([grad_kv_own, grad_q_rows], axis=1).astype(LOW)

    grad_normed_part = dot(grad_qkv, w_all[:, : 3 * gw], ((1,), (1,)))
    grad_low = grad_normed_part.astype(LOW).reshape(Z, own_rows, D)
    grad_normed_one = grad_normed_part[:own_rows]
    for d in range(1, Z):
        grad_normed_one = grad_normed_one + shift(grad_low[d], "hz", -d).astype(WIDE)
    def pad_columns(columns):
        return jnp.pad(columns, ((0, 0), (0, 128 - columns.shape[1])))

    attn_part = jnp.concatenate(
        [grad_attn_out, pad_columns(jnp.concatenate([grad_gain_two[:, None], grad_router], 1))],
        axis=1,
    )
    me_c = lax.axis_index("cc")
    cores = lax.axis_size("cc")
    yx = Y * E // cores

    def to_chip(part):
        split = part.astype(LOW).reshape(Z, yx, cores, shard, part.shape[1])
        split = split.transpose(2, 1, 0, 3, 4).reshape(cores, yx, Z * shard, part.shape[1])
        other = swap(pick(split, 1 - me_c), ("cc",), 1)
        return (pick(split, me_c).astype(WIDE) + other.astype(WIDE)).astype(LOW)

    attn_chip = to_chip(attn_part)

    line_rows = Z * shard
    table_size = 3 * hg * buckets

    def table_columns(table, rows):
        width = -(-table_size // rows)
        terms = jnp.pad(low_terms(table).reshape(-1), (0, rows * width - table_size))
        return terms.reshape(rows, width)

    def table_of(columns):
        terms = columns.reshape(columns.shape[0], -1)[:, :table_size]
        return terms.reshape(-1, 3, hg, buckets).sum(axis=1)

    grad_w_qkv = dot(normed_one, grad_qkv, ((0,), (0,))).astype(LOW)
    table_chip = table_part + swap(table_part, ("cc",), 1)
    table_block = table_columns(table_chip, line_rows)
    table_width = table_block.shape[1]
    extra_width = -(-(3 * gw + table_width) // 128) * 128 - 3 * gw
    table_block = jnp.pad(table_block, ((0, 0), (0, extra_width - table_width)))
    extra = jnp.broadcast_to(table_block[None], (yx, line_rows, extra_width))
    attn_width = attn_part.shape[1]
    chip_blocks = jnp.concatenate([attn_chip, to_chip(grad_w_qkv), extra], axis=2)
    got = every_block(chip_blocks, ("yy", "xx")).astype(WIDE)
    layer_sum = got[:, :, : attn_width + 3 * gw].sum(axis=0)
    attn_sum, qkv_sum = layer_sum[:, :attn_width], layer_sum[:, attn_width:]
    table_at = attn_width + 3 * gw
    layer_table = table_of(got[:, :, table_at : table_at + table_width]).sum(axis=0)
    first_low = first_low.reshape(Y, D // N, FF // Y)
    first_sent = [pick(first_low, y ^ k) for k in range(1, Y)]
    first_got = [swap(sent, ("yy",), k) for k, sent in enumerate(first_sent, 1)]
    first_parts = from_xor([pick(first_low, y)] + first_got, y)
    table_block = after(table_columns(layer_table, shard), grad_low, *first_sent)
    line_width = table_block.shape[1]
    grad_normed_one = after(grad_normed_one, *first_got)
    own_hat = hat_one[:own_rows]
    grad_hat_one = grad_normed_one * gain_first
    grad_inputs = grad_resid + scale_one[:own_rows] * (
        grad_hat_one - own_hat * jnp.mean(grad_hat_one * own_hat, axis=-1, keepdims=True)
    )
    line_blocks = jnp.concatenate(
        [
            attn_sum.astype(LOW).reshape(Z, shard, attn_width),
            qkv_sum.astype(LOW).reshape(Z, shard, 3 * gw),
            jnp.broadcast_to(table_block[None], (Z, shard, line_width)),
        ],
        axis=2,
    )
    line_pad = -(-line_blocks.shape[2] // 128) * 128 - line_blocks.shape[2]
    line_blocks = jnp.pad(line_blocks, ((0, 0), (0, 0), (0, line_pad)))
    line = every_block(line_blocks, ("hz",)).astype(WIDE)
    attn_total = line[:, :, :attn_width].sum(axis=0)
    shard_attn_out = attn_total[:, :D]
    shard_gain_two = attn_total[:, D]
    shard_router = attn_total[:, D + 1 : D + 1 + E]
    line = line[:, :, attn_width:]
    shard_qkv = jnp.concatenate(
        [line[g, :, part * gw : (part + 1) * gw] for part in (2, 0, 1) for g in range(Z)], axis=1
    )
    shard_gain_one = jnp.sum(
        shard_qkv * query_key_value_weight.astype(WIDE), axis=1
    ) / gain_one.astype(WIDE)
    tables = table_of(line[:, :, 3 * gw : 3 * gw + line_width])
    table_total = tables.reshape(heads, buckets).T

    shard_second = after(shard_second, table_block).astype(WIDE)
    shard_first = jnp.concatenate(
        [
            first_parts[k][:, g * part_ff : (g + 1) * part_ff]
            for g in range(Z)
            for k in range(Y)
        ],
        axis=1,
    ).astype(WIDE)
    return (
        output[None],
        grad_inputs[None],
        shard_gain_one,
        shard_qkv,
        shard_attn_out,
        table_total,
        shard_gain_two,
        shard_router,
        shard_first[None],
        shard_second[None],
    )


def solution(mesh):
    devices_ctx, devices_exp = mesh.shape["ctx"], mesh.shape["exp"]
    outer = 4
    parts = Mesh(
        mesh.devices.reshape(outer, devices_ctx // outer, devices_exp // 2, 2),
        ("hz", "yy", "xx", "cc"),
    )
    ctx, exp = ("hz", "yy"), ("xx", "cc")
    every = ctx + exp
    tokens = P(exp, ctx, None)
    return jax.shard_map(
        body,
        mesh=parts,
        in_specs=(
            tokens,
            P(every),
            P(every, None),
            P(every, None),
            P(),
            P(every),
            P(every, None),
            tokens,
            tokens,
            tokens,
            P(),
            tokens,
        ),
        out_specs=(
            tokens,
            tokens,
            P(every),
            P(every, None),
            P(every, None),
            P(),
            P(every),
            P(every, None),
            tokens,
            tokens,
        ),
        check_vma=False,
    )
```
